32 devices in a mesh: tm: 16 (over z, y, x), sens: 2 (over core).
Axes of the slice: x: 2, y: 2, z: 4, core: 2. Of those that a mesh axis runs over, the one named last changes fastest.
Arguments:
- telemetry: float32 [8192, 512], P('tm', 'sens'), may hold values from -6 to 6
- present: int32 [512, 8], P('tm', 'sens'), may hold values 0 or 1
- transition: float32 [128, 128], replicated, may hold values from -1 to 1, as said below
- sensing: float32 [512, 128], P('sens'), may hold values from -3 to 3, as said below
- filter_gain: float32 [128, 512], P(None, 'sens'), may hold values from -1 to 1, as said below
- smooth_gain: float32 [128, 128], replicated, may hold values from -1 to 1, as said below
- initial_state: float32 [128], replicated, may hold values from -6 to 6
Outputs:
- new_transition: float32 [128, 128], replicated
- new_sensing: float32 [512, 128], P('sens')
- smoothed: float32 [8192, 128], P('tm')
The draws below stay inside these ranges and needn't reach their ends.
Inputs may be any that keep to these rules, and one draw needn't show every extreme that they name: `transition`: the previous iteration's estimate of the transition matrix; every entry lies between -1 and 1. `sensing`: the previous iteration's estimate of the observation matrix; every entry lies between -3 and 3. `filter_gain`: the previous iteration's steady filter gain; every entry lies between -1 and 1. `smooth_gain`: the previous iteration's steady smoother gain; every entry lies between -1 and 1.
All inputs are finite; a program needn't handle non-finite values. No bound on the sum of `present` on one device may be relied on, other than what follows from the above.
Results may differ from the reference program's by a relative error of at most 0.014.
Values sent between devices are 32-bit elements; how exact they have to be, the bound alone decides.
A program may use at most 128 MiB of HBM per device.

```python
import math
import jax
import jax.numpy as jnp
from jax import lax

S = 128
NS = 512
NB = 8
SEG = 16
TM_DEV = 512
STEPS = 8192


def slow_channels(key):
    slow_count = S // 2
    ranking = jax.random.permutation(jax.random.fold_in(key, 101), S)
    slow_mask = ranking < slow_count
    fast_count = float(S - slow_count)
    return (slow_mask, fast_count, float(slow_count))


def slow_rotation(key, slow_mask, slow_count):
    noise = jax.random.truncated_normal(key, -3.0, 3.0, (S, S), jnp.float32)
    skew = (noise - noise.T) * (0.5 / (TM_DEV * math.sqrt(2.0 * slow_count)))
    slow_pair = jnp.logical_and(slow_mask[:, None], slow_mask[None, :])
    return jnp.where(slow_pair, skew, 0.0)


def state_matrix(key, tag, low_rate, high_rate):
    slow_mask, fast_count, slow_count = slow_channels(key)
    subkeys = jax.random.split(jax.random.fold_in(key, tag), 4)
    spread = jnp.exp(jax.random.uniform(subkeys[0], (S,), jnp.float32, math.log(0.2), math.log(2.0)))
    slow_rate = jnp.exp(-spread / STEPS)
    fast_rate = jax.random.uniform(subkeys[1], (S,), jnp.float32, low_rate, high_rate)
    noise = jax.random.truncated_normal(subkeys[2], -3.0, 3.0, (S, S), jnp.float32)
    diagonal = jnp.eye(S, dtype=bool)
    slow_row = slow_mask[:, None]
    fast_col = jnp.logical_not(slow_mask)[None, :]
    fast_pair = jnp.logical_and(jnp.logical_and(jnp.logical_not(slow_row), fast_col), jnp.logical_not(diagonal))
    slow_fast = jnp.logical_and(slow_row, fast_col)
    rates = jnp.where(slow_mask, slow_rate, fast_rate)
    result = jnp.where(diagonal, rates[None, :], 0.0)
    result = result + jnp.where(fast_pair, noise * (0.15 / math.sqrt(fast_count)), 0.0)
    result = result + jnp.where(slow_fast, noise * (0.5 / math.sqrt(fast_count * STEPS)), 0.0)
    result = result + slow_rotation(subkeys[3], slow_mask, slow_count)
    return result.astype(jnp.float32)


def draw_transition(key, part):
    return state_matrix(key, 1, 0.3, 0.55)


def draw_sensing(key, part):
    slow_mask, fast_count, slow_count = slow_channels(key)
    noise = jax.random.truncated_normal(jax.random.fold_in(key, 2), -3.0, 3.0, (NS, S), jnp.float32)
    column_scale = jnp.where(slow_mask, 1.0 / math.sqrt(slow_count * STEPS), 1.0 / math.sqrt(fast_count))
    return (noise * column_scale[None, :]).astype(jnp.float32)


def draw_filter_gain(key, part):
    slow_mask, fast_count, slow_count = slow_channels(key)
    noise = jax.random.truncated_normal(jax.random.fold_in(key, 3), -3.0, 3.0, (S, NS), jnp.float32)
    row_scale = jnp.where(slow_mask, 1.0 / math.sqrt(NS * STEPS), 0.08 / math.sqrt(NS))
    return (noise * row_scale[:, None]).astype(jnp.float32)


def draw_smooth_gain(key, part):
    return state_matrix(key, 4, 0.2, 0.45)


def place_ends(values, rng, least, top_value):
    dims = values.shape
    index_at = [jax.random.randint(jax.random.fold_in(rng, axis), (), 0, dims[axis]) for axis in range(len(dims))]
    values = values.at[tuple(index_at)].set(least)
    longest = dims.index(max(dims))
    index_at[longest] = (index_at[longest] + 1) % dims[longest]
    return values.at[tuple(index_at)].set(top_value)


def shard_levels(stream_key, extent, pieces, smallest, top_value):
    def one(dim, parts):
        draws = jax.random.uniform(jax.random.fold_in(jax.random.fold_in(stream_key, 6), dim), (parts,), jnp.float32, smallest / len(pieces), top_value / len(pieces))
        return jnp.repeat(jnp.exp(draws), extent[dim] // parts).reshape((-1,) + (1,) * (len(extent) - dim - 1))

    level = one(*pieces[0])
    for cut in pieces[1:]:
        level = level * one(*cut)
    return level


def scatter_about(own_key, extent, scale, bound, pieces=(), kind=jnp.bfloat16):
    drawn = jax.random.normal(own_key, extent, jnp.float32) * scale
    if len(pieces) > 0:
        drawn = shard_levels(own_key, extent, pieces, -0.22, 0.18) * drawn
    return jnp.clip(drawn, min=-bound, max=bound).astype(kind)


def setup_inputs(seed: int = 0) -> dict:
    streams_of = jax.random.split(jax.random.key(seed), 8)
    return {
        "telemetry": scatter_about(streams_of[0], (STEPS, NS), 1.0, 6.0, ((0, 16), (1, 2)), jnp.float32),
        "present": place_ends((jax.random.randint(streams_of[1], (STEPS // SEG, NB), 0, 4) < 3).astype(jnp.int32), jax.random.fold_in(streams_of[1], 1), 0, 1),
        "transition": draw_transition(jax.random.fold_in(streams_of[7], 71), 0),
        "sensing": draw_sensing(jax.random.fold_in(streams_of[7], 71), 0),
        "filter_gain": draw_filter_gain(jax.random.fold_in(streams_of[7], 71), 0),
        "smooth_gain": draw_smooth_gain(jax.random.fold_in(streams_of[7], 71), 0),
        "initial_state": scatter_about(streams_of[6], (S,), 1.0, 6.0, (), jnp.float32),
    }


HIGHEST = lax.Precision.HIGHEST
RIDGE = 0.001

def solve_rows(gram, cross, ridge_term):
    factor = jnp.linalg.cholesky(gram + ridge_term * jnp.eye(gram.shape[0], dtype=jnp.float32))
    return jax.scipy.linalg.cho_solve((factor, True), cross.T).T

def reference(telemetry, present, transition, sensing, filter_gain, smooth_gain, initial_state):
    block_size = NS // NB
    step_flags = jnp.repeat(present.astype(jnp.float32), SEG, axis=0)

    def forward(carried, step_input):
        observed, flag_row = step_input
        predicted = jnp.dot(transition, carried, precision=HIGHEST)
        sensor_flags = jnp.repeat(flag_row, block_size)
        residual = sensor_flags * (observed - jnp.dot(sensing, predicted, precision=HIGHEST))
        updated = predicted + jnp.dot(filter_gain, residual, precision=HIGHEST)
        return (updated, updated)
    unused_last, filtered = lax.scan(forward, initial_state.astype(jnp.float32), (telemetry, step_flags))
    mixing = jnp.dot(smooth_gain, transition, precision=HIGHEST)
    drives = filtered - jnp.dot(filtered, mixing.T, precision=HIGHEST)

    def backward(following, drive_row):
        current = jnp.dot(smooth_gain, following, precision=HIGHEST) + drive_row
        return (current, current)
    final_state = jnp.dot(transition, filtered[-1], precision=HIGHEST)
    unused_first, smoothed = lax.scan(backward, final_state, drives, reverse=True)
    ridge_term = RIDGE * STEPS
    earlier_rows = smoothed[:-1]
    later_rows = smoothed[1:]
    lag_gram = jnp.dot(earlier_rows.T, earlier_rows, precision=HIGHEST)
    lag_cross = jnp.dot(later_rows.T, earlier_rows, precision=HIGHEST)
    new_transition = solve_rows(lag_gram, lag_cross, ridge_term)
    masked = telemetry * jnp.repeat(step_flags, block_size, axis=1)

    def block_update(block_index):
        block_flags = lax.dynamic_index_in_dim(step_flags, block_index, 1, keepdims=False)
        block_gram = jnp.dot((smoothed * block_flags[:, None]).T, smoothed, precision=HIGHEST)
        block_rows = lax.dynamic_slice_in_dim(masked, block_index * block_size, block_size, 1)
        block_cross = jnp.dot(block_rows.T, smoothed, precision=HIGHEST)
        return solve_rows(block_gram, block_cross, ridge_term)
    new_sensing = lax.map(block_update, jnp.arange(NB, dtype=jnp.int32)).reshape(NS, S)
    return (new_transition, new_sensing, smoothed)
```

```python
import functools

import jax
import jax.numpy as jnp
from jax import lax
from jax.experimental import pallas as pl
from jax.experimental.pallas import tpu as pltpu
from jax.sharding import PartitionSpec as P

RIDGE = 0.001
GROUP = 4
PIVOT = 16
MESH = pl.DeviceIdType.MESH
VMEM = pltpu.VMEM
F32 = jnp.float32
LIMIT = 48 * 1024 * 1024


def mm(a, b):
    return jnp.dot(a, b, precision=lax.Precision.HIGHEST, preferred_element_type=F32)


def mm_tn(a, b):
    return lax.dot_general(
        a, b, (((0,), (0,)), ((), ())),
        precision=lax.Precision.HIGHEST, preferred_element_type=F32,
    )


def mm_nt(a, b):
    return lax.dot_general(
        a, b, (((1,), (1,)), ((), ())),
        precision=lax.Precision.HIGHEST, preferred_element_type=F32,
    )


def row_ids(shape):
    return lax.broadcasted_iota(jnp.int32, shape, 0)


def shift_down(v, by):
    if by % 8 == 0:
        return jnp.concatenate([jnp.zeros((by, v.shape[1]), F32), v[:-by]], axis=0)
    return jnp.where(row_ids(v.shape) >= by, pltpu.roll(v, by, 0), 0.0)


def shift_up(v, by):
    rows = v.shape[0]
    if by % 8 == 0:
        return jnp.concatenate([v[by:], jnp.zeros((by, v.shape[1]), F32)], axis=0)
    return jnp.where(row_ids(v.shape) < rows - by, pltpu.roll(v, rows - by, 0), 0.0)


def vmem_call(body, out_shape, scratch=(), in_specs=None, remote=None):
    params = dict(vmem_limit_bytes=LIMIT)
    if remote is not None:
        params.update(collective_id=remote, has_side_effects=True)
    return pl.pallas_call(
        body,
        out_shape=out_shape,
        in_specs=in_specs,
        out_specs=jax.tree.map(lambda _: pl.BlockSpec(memory_space=VMEM), out_shape),
        scratch_shapes=list(scratch),
        compiler_params=pltpu.CompilerParams(**params),
    )


def in_vmem(count):
    return [pl.BlockSpec(memory_space=VMEM)] * count


def shaped(*shape):
    return jax.ShapeDtypeStruct(shape, F32)


def push_kernel(tele, flags, trans, sense, gain, masked, push, corr):
    rows, sensors = tele.shape
    segs, blocks = flags.shape
    seg_len, width = rows // segs, sensors // blocks
    spread = jnp.where(
        lax.broadcasted_iota(jnp.int32, (blocks, sensors), 1) // width
        == lax.broadcasted_iota(jnp.int32, (blocks, sensors), 0), 1.0, 0.0)
    wide = jnp.dot(flags[...], spread, preferred_element_type=F32)
    step = jnp.broadcast_to(wide[:, None, :], (segs, seg_len, sensors)).reshape(rows, sensors)
    values = tele[...] * step
    masked[...] = values
    push[...] = mm_nt(values, gain[...])
    moved = mm(sense[...], trans[...])
    for g in range(blocks):
        part = slice(g * width, (g + 1) * width)
        corr[g] = lax.dot_general(
            moved[part], gain[:, part], (((0,), (1,)), ((), ())),
            precision=lax.Precision.HIGHEST, preferred_element_type=F32)


def remote(src, dst, send, recv, where):
    return pltpu.make_async_remote_copy(
        src_ref=src, dst_ref=dst, send_sem=send, recv_sem=recv,
        device_id=where, device_id_type=MESH)


def pair_kernel(push, corr, flags, push_in, corr_in, flags_in, send, recv):
    tm, core = lax.axis_index("tm"), lax.axis_index("sens")
    other = (tm, 1 - core)
    barrier = pltpu.get_barrier_semaphore()
    pl.semaphore_signal(barrier, inc=1, device_id=other, device_id_type=MESH)
    pl.semaphore_wait(barrier, 1)
    half = push.shape[0] // 2
    theirs = pl.ds(pl.multiple_of((1 - core) * half, half), half)
    copies = [
        remote(corr, corr_in, send.at[0], recv.at[0], other),
        remote(push.at[theirs], push_in, send.at[1], recv.at[1], other),
        remote(flags, flags_in, send.at[2], recv.at[2], other),
    ]
    for copy in copies:
        copy.start()
    for copy in copies:
        copy.wait()


def maps_kernel(seg_len, push, push_in, corr, corr_in, flags, flags_in, trans,
                powers, ends, local, chunk, tree):
    core = lax.axis_index("sens")
    segs = ends.shape[0]
    width = trans.shape[0]
    blocks = corr.shape[0]
    levels = seg_len.bit_length() - 1

    def one(k):
        row = core * segs + k
        q = trans[...].T
        for g in range(blocks):
            q = q - flags[row, g] * corr[g] - flags_in[row, g] * corr_in[g]
        mine = pl.ds(pl.multiple_of(row * seg_len, seg_len), seg_len)
        here = pl.ds(pl.multiple_of(k * seg_len, seg_len), seg_len)
        v = push[mine] + push_in[here]
        for s in range(levels):
            powers[s, k] = q
            t = mm(jnp.concatenate([q, v], axis=0), q)
            v = v + shift_down(t[width:], 1 << s)
            q = t[:width]
        local[here] = v
        ends[k] = q
        tree[k, :width] = q
        tree[k, width:] = jnp.broadcast_to(v[seg_len - 1:], (8, width))

    unroll = 4

    def several(i, carry):
        for j in range(unroll):
            one(i * unroll + j)
        return carry

    lax.fori_loop(0, segs // unroll, several, 0)
    span = 1
    while span < segs:
        for k in range(0, segs, 2 * span):
            tree[k] = compose(tree[k], tree[k + span])
        span *= 2
    chunk[...] = tree[0]


def compose(first, second):
    width = second.shape[1]
    t = mm(first, second[:width])
    return jnp.concatenate([t[:width], t[width:] + second[width:]], axis=0)


def follow(x, step):
    width = step.shape[1]
    return mm(x, step[:width]) + step[width:]


def carry_kernel(n, chunk, start, entry, pair, chip, group, arrived, leaving, send, recv):
    tm, core = lax.axis_index("tm"), lax.axis_index("sens")
    place, mine = lax.rem(tm, GROUP), lax.div(tm, GROUP)
    groups = n // GROUP
    other = (tm, 1 - core)
    base = tm - place
    peers = [(base + lax.rem(place + k, GROUP), core) for k in range(1, GROUP)]
    barrier = pltpu.get_barrier_semaphore()
    chain = [(lax.rem(tm + by, n), core) for by in (GROUP, n - GROUP)]
    for peer in [other] + peers + chain:
        pl.semaphore_signal(barrier, inc=1, device_id=peer, device_id_type=MESH)
    pl.semaphore_wait(barrier, GROUP + 2)

    swap = remote(chunk, pair, send.at[0], recv.at[0], other)
    swap.start()
    swap.wait()
    own, their = chunk[...], pair[...]
    first = jnp.where(core == 0, own, their)
    chip[...] = compose(first, jnp.where(core == 0, their, own))
    copies = []
    for k, peer in enumerate(peers):
        copy = remote(chip, group.at[k], send.at[1 + k], recv.at[1 + k], peer)
        copy.start()
        copies.append(copy)
    for copy in copies:
        copy.wait()
    held = [chip[...]] + [group[k] for k in range(GROUP - 1)]
    ordered = []
    for p in range(GROUP):
        value = held[0]
        for k in range(1, GROUP):
            value = jnp.where(lax.rem(place - k + GROUP, GROUP) == p, held[k], value)
        ordered.append(value)
    low, high = compose(ordered[0], ordered[1]), compose(ordered[2], ordered[3])
    whole = compose(low, high)
    hand = remote(leaving, arrived, send.at[GROUP], recv.at[GROUP], (tm + GROUP, core))

    @pl.when(mine == 0)
    def _():
        arrived[...] = start[...]

    @pl.when(mine > 0)
    def _():
        remote(leaving, arrived, send.at[GROUP], recv.at[GROUP], (tm - GROUP, core)).wait_recv()

    x = arrived[...]
    leaving[...] = follow(x, whole)

    @pl.when(mine < groups - 1)
    def _():
        hand.start()

    x = jnp.where(place >= 2, follow(x, low), x)
    before = jnp.where(place >= 2, ordered[2], ordered[0])
    x = jnp.where(lax.rem(place, 2) == 1, follow(x, before), x)
    entry[...] = jnp.where(core == 1, follow(x, first), x)

    @pl.when(mine < groups - 1)
    def _():
        hand.wait_send()


def filter_kernel(n, seg_len, entry, powers, ends, local, trans, smooth,
                  drive_scan, gains, shift, final, states, filtered):
    levels, segs = powers.shape[:2]
    width = trans.shape[0]
    rows = segs * seg_len

    x = entry[...]
    for k in range(segs):
        states[k] = x
        x = mm(x, ends[k]) + local[(k + 1) * seg_len - 1:(k + 1) * seg_len]

    def one(k):
        here = pl.ds(pl.multiple_of(k * seg_len, seg_len), seg_len)
        w = jnp.concatenate([states[k]] * (seg_len // 8), axis=0)
        ids = row_ids(w.shape)
        for s in range(levels):
            w = jnp.where((ids // (1 << s)) % 2 == 1, mm(w, powers[s, k]), w)
        filtered[here] = local[here] + mm(w, powers[0, k])

    unroll = 4

    def several(i, carry):
        for j in range(unroll):
            one(i * unroll + j)
        return carry

    lax.fori_loop(0, segs // unroll, several, 0)
    f = filtered[...]
    ahead = mm_nt(f, trans[...])
    v = f - mm_nt(ahead, smooth[...])
    last = jnp.broadcast_to(ahead[rows - 1:], (8, width))
    final[...] = last
    p = smooth[...].T
    span, level = 1, 0
    while span < rows:
        gains[level] = p
        t = mm(jnp.concatenate([p, v], axis=0), p)
        v = v + shift_up(t[width:], span)
        p = t[:width]
        span, level = span * 2, level + 1
    gains[level] = p
    drive_scan[...] = v
    is_last = (lax.axis_index("tm") == n - 1) & (lax.axis_index("sens") == 1)
    s = jnp.broadcast_to(v[:1], (8, width))
    shift[...] = jnp.where(is_last, s + mm(last, p), s)


def smooth_kernel(n, drive_scan, gains, shift, final, out, entry, shifts, send, recv):
    tm, core = lax.axis_index("tm"), lax.axis_index("sens")
    chunks = 2 * n
    me = tm * 2 + core
    half, width = drive_scan.shape
    barrier = pltpu.get_barrier_semaphore()

    def place(k):
        c = lax.rem(me + k, chunks)
        return (lax.div(c, 2), lax.rem(c, 2))

    def greet(k, carry):
        pl.semaphore_signal(barrier, inc=1, device_id=place(k), device_id_type=MESH)
        return carry

    lax.fori_loop(1, chunks, greet, 0)
    pl.semaphore_wait(barrier, chunks - 1)

    def launch(k, carry):
        remote(shift, shifts.at[me], send.at[k], recv.at[me], place(k)).start()
        return carry

    lax.fori_loop(1, chunks, launch, 0)
    shifts[me] = shift[...]

    def land(k, carry):
        c = lax.rem(me + k, chunks)
        remote(shift, shifts.at[c], send.at[k], recv.at[c], place(k)).wait()
        return carry

    lax.fori_loop(1, chunks, land, 0)
    v = shifts[:, 0, :]
    levels = gains.shape[0] - 1
    p = gains[levels]
    span = 1
    while span < chunks:
        t = mm(jnp.concatenate([p, v], axis=0), p)
        v = v + shift_up(t[width:], span)
        p = t[:width]
        span *= 2
    x = jnp.sum(jnp.where(row_ids(v.shape) == me + 1, v, 0.0), axis=0, keepdims=True)
    x = jnp.where(me == chunks - 1, final[...], jnp.broadcast_to(x, (8, width)))
    after = jnp.where(row_ids(v.shape) == 2 * tm + 2, v, 0.0)
    entry[...] = jnp.broadcast_to(jnp.sum(after, axis=0, keepdims=True), (8, width))
    w = x
    ids = 7 - row_ids(w.shape)
    for s in range(3):
        w = jnp.where((ids // (1 << s)) % 2 == 1, mm(w, gains[s]), w)
    w = mm(w, gains[0])
    for s in range(3, levels):
        w = jnp.concatenate([mm(w, gains[s]), w], axis=0)
    mine = pl.ds(pl.multiple_of(core * half, half), half)
    out[mine] = drive_scan[...] + w
    swap = remote(out.at[mine], out.at[mine], send.at[0], recv.at[chunks], (tm, 1 - core))
    swap.start()
    swap.wait()


def stats_kernel(n, smoothed, entry, masked, flags, stats):
    rows, width = smoothed.shape
    segs, blocks = flags.shape
    seg_len = rows // segs
    sensors = masked.shape[1]
    tm, core = lax.axis_index("tm"), lax.axis_index("sens")
    x = smoothed[...]
    ids = row_ids((rows, width))
    weight = jnp.where((tm == n - 1) & (ids == rows - 1), 0.0, 1.0)
    prior = x * weight
    above = pltpu.roll(x, rows - 1, 0)
    above = jnp.where(ids == rows - 1, jnp.broadcast_to(entry[:1], (rows, width)), above)
    stats[:width] = mm_tn(prior, x)
    stats[(blocks + 1) * width:(blocks + 2) * width] = mm_tn(above, prior)
    for g in range(blocks):
        column = jnp.broadcast_to(flags[:, g:g + 1], (segs, width))
        step = jnp.broadcast_to(column[:, None, :], (segs, seg_len, width)).reshape(rows, width)
        stats[(g + 1) * width:(g + 2) * width] = mm_tn(x * step, x)
    stats[(blocks + 2) * width:] = mm_tn(masked[...], x)


def sum_kernel(n, stats, total, parts, send, recv, send2, recv2):
    me, core = lax.axis_index("tm"), lax.axis_index("sens")
    piece = stats.shape[0] // n
    barrier = pltpu.get_barrier_semaphore()

    def at(c):
        return pl.ds(pl.multiple_of(c * piece, piece), piece)

    def peer(k):
        return lax.rem(me + k, n)

    def greet(k, carry):
        pl.semaphore_signal(barrier, inc=1, device_id=(peer(k), core), device_id_type=MESH)
        return carry

    lax.fori_loop(1, n, greet, 0)
    pl.semaphore_wait(barrier, n - 1)

    def scatter(k, carry):
        c = peer(k)
        remote(stats.at[at(c)], parts.at[me], send.at[k], recv.at[me], (c, core)).start()
        return carry

    lax.fori_loop(1, n, scatter, 0)
    parts[me] = stats[at(me)]

    def land(k, carry):
        c = peer(k)
        remote(stats.at[at(c)], parts.at[c], send.at[k], recv.at[c], (c, core)).wait()
        return carry

    lax.fori_loop(1, n, land, 0)
    total[at(me)] = jnp.sum(parts[...], axis=0)

    def spread(k, carry):
        c = peer(k)
        remote(total.at[at(me)], total.at[at(me)], send2.at[k], recv2.at[me], (c, core)).start()
        return carry

    lax.fori_loop(1, n, spread, 0)

    def close(k, carry):
        c = peer(k)
        remote(total.at[at(me)], total.at[at(c)], send2.at[k], recv2.at[c], (c, core)).wait()
        return carry

    lax.fori_loop(1, n, close, 0)


def inverse_factor(a):
    count, size = a.shape[:2]
    shape = (count, size, 2 * size)
    rows = lax.broadcasted_iota(jnp.int32, shape, 1)
    cols = lax.broadcasted_iota(jnp.int32, shape, 2)
    a = jnp.concatenate([a, jnp.where(rows + size == cols, 1.0, 0.0)[:, :, size:]], axis=2)
    for k in range(size):
        scale = 1.0 / jnp.sqrt(a[:, k:k + 1, k:k + 1])
        r = a[:, k:k + 1, :] * scale
        c = jnp.where(rows > k, a[:, :, k:k + 1] * scale, 0.0)
        a = jnp.where(rows == k, r, a - c * r)
    return a[:, :, size:]


def solve_kernel(ridge, stats, new_transition, new_sensing, work):
    width = stats.shape[1]
    sensors = new_sensing.shape[0]
    count = (stats.shape[0] - sensors) // width - 1
    size = sensors // (count - 1)
    eye = jnp.where(
        row_ids((width, width)) == lax.broadcasted_iota(jnp.int32, (width, width), 1), ridge, 0.0)
    cross = count * width
    for s in range(count):
        work[s, :, :width] = stats[s * width:(s + 1) * width] + eye
    work[0, :, width:] = stats[cross:cross + width].T
    for s in range(1, count):
        at = cross + width + (s - 1) * size
        block = stats[at:at + size].T
        work[s, :, width:] = jnp.concatenate([block] * (width // size), axis=1)
    steps = width // PIVOT
    inverses = []
    for j in range(steps):
        lo, hi = j * PIVOT, (j + 1) * PIVOT
        inv = inverse_factor(jnp.stack([work[s, lo:hi, lo:hi] for s in range(count)]))
        inverses.append(inv)
        for s in range(count):
            row = mm(inv[s], work[s, lo:hi, :])
            work[s, lo:hi, :] = row
            if hi < width:
                work[s, hi:, :] = work[s, hi:, :] - mm_tn(row[:, hi:width], row)
    for s in range(count):
        x = None
        for j in reversed(range(steps)):
            lo, hi = j * PIVOT, (j + 1) * PIVOT
            rhs = work[s, lo:hi, width:]
            if x is not None:
                rhs = rhs - mm(work[s, lo:hi, hi:width], x)
            piece = mm_tn(inverses[j][s], rhs)
            x = piece if x is None else jnp.concatenate([piece, x], axis=0)
        if s == 0:
            new_transition[...] = x.T
        else:
            new_sensing[(s - 1) * size:s * size] = x.T[:size]


def on_device(n, telemetry, present, transition, sensing, filter_gain, smooth_gain, initial_state):
    width = transition.shape[0]
    rows, sensors = telemetry.shape
    segs, blocks = present.shape
    seg_len = rows // segs
    half, half_segs = rows // 2, segs // 2
    dma = pltpu.SemaphoreType.DMA
    flags = present.astype(F32)
    wide_flags = jnp.pad(flags, ((0, 0), (0, 128 - blocks)))
    start = jnp.broadcast_to(initial_state[None], (8, width))

    masked, push, corr = vmem_call(
        push_kernel,
        (shaped(rows, sensors), shaped(rows, width), shaped(blocks, width, width)),
        in_specs=in_vmem(5),
    )(telemetry, flags, transition, sensing, filter_gain)
    push_in, corr_in, flags_in = vmem_call(
        pair_kernel,
        (shaped(half, width), shaped(blocks, width, width), shaped(segs, 128)),
        [dma((3,)), dma((3,))],
        in_vmem(3), remote=1,
    )(push, corr, wide_flags)
    levels = seg_len.bit_length() - 1
    scalars = pl.BlockSpec(memory_space=pltpu.SMEM)
    powers, ends, local, chunk = vmem_call(
        functools.partial(maps_kernel, seg_len),
        (shaped(levels, half_segs, width, width), shaped(half_segs, width, width),
         shaped(half, width), shaped(width + 8, width)),
        [VMEM((half_segs, width + 8, width), F32)],
        in_vmem(4) + [scalars, scalars] + in_vmem(1),
    )(push, push_in, corr, corr_in, wide_flags, flags_in, transition)
    entry = vmem_call(
        functools.partial(carry_kernel, n),
        shaped(8, width),
        [VMEM((width + 8, width), F32), VMEM((width + 8, width), F32),
         VMEM((GROUP - 1, width + 8, width), F32), VMEM((8, width), F32), VMEM((8, width), F32),
         dma((GROUP + 1,)), dma((GROUP + 1,))],
        in_vmem(2), remote=2,
    )(chunk, start)
    back_levels = half.bit_length() - 1
    drive_scan, gains, shift, final = vmem_call(
        functools.partial(filter_kernel, n, seg_len),
        (shaped(half, width), shaped(back_levels + 1, width, width), shaped(8, width),
         shaped(8, width)),
        [VMEM((half_segs, 8, width), F32), VMEM((half, width), F32)],
        in_vmem(6),
    )(entry, powers, ends, local, transition, smooth_gain)
    smoothed, entry_back = vmem_call(
        functools.partial(smooth_kernel, n),
        (shaped(rows, width), shaped(8, width)),
        [VMEM((2 * n, 8, width), F32), dma((2 * n,)), dma((2 * n + 1,))],
        in_vmem(4), remote=3,
    )(drive_scan, gains, shift, final)
    stats = vmem_call(
        functools.partial(stats_kernel, n),
        shaped((blocks + 2) * width + sensors, width),
        in_specs=in_vmem(4),
    )(smoothed, entry_back, masked, flags)
    total = vmem_call(
        functools.partial(sum_kernel, n),
        shaped(*stats.shape),
        [VMEM((n, stats.shape[0] // n, width), F32), dma((n,)), dma((n,)), dma((n,)), dma((n,))],
        in_vmem(1), remote=4,
    )(stats)
    new_transition, new_sensing = vmem_call(
        functools.partial(solve_kernel, RIDGE * rows * n),
        (shaped(width, width), shaped(sensors, width)),
        [VMEM((blocks + 1, width, 2 * width), F32)],
        in_vmem(1),
    )(total)
    return (new_transition, new_sensing, smoothed)


def solution(mesh):
    placed = (P("tm", "sens"), P("tm", "sens"), P(), P("sens", None), P(None, "sens"), P(), P())
    return jax.shard_map(
        functools.partial(on_device, mesh.shape["tm"]),
        mesh=mesh,
        in_specs=placed,
        out_specs=(P(), P("sens", None), P("tm", None)),
        check_vma=False,
    )
```

```python
import functools

import jax
import jax.numpy as jnp
from jax import lax
from jax.experimental import pallas as pl
from jax.experimental.pallas import tpu as pltpu
from jax.sharding import PartitionSpec as P

RIDGE = 0.001
GROUP = 4
PIVOT = 32
MESH = pl.DeviceIdType.MESH
VMEM = pltpu.VMEM
F32 = jnp.float32
LIMIT = 48 * 1024 * 1024


def mm(a, b):
    return jnp.dot(a, b, precision=lax.Precision.HIGHEST, preferred_element_type=F32)


def mv(a, b):
    return jnp.dot(a, b, precision=lax.Precision.HIGH, preferred_element_type=F32)


def mm_tn(a, b):
    return lax.dot_general(
        a, b, (((0,), (0,)), ((), ())),
        precision=lax.Precision.HIGHEST, preferred_element_type=F32,
    )


def mm_nt(a, b):
    return lax.dot_general(
        a, b, (((1,), (1,)), ((), ())),
        precision=lax.Precision.HIGHEST, preferred_element_type=F32,
    )


def row_ids(shape):
    return lax.broadcasted_iota(jnp.int32, shape, 0)


def shift_down(v, by):
    if by % 8 == 0:
        return jnp.concatenate([jnp.zeros((by, v.shape[1]), F32), v[:-by]], axis=0)
    return jnp.where(row_ids(v.shape) >= by, pltpu.roll(v, by, 0), 0.0)


def shift_up(v, by):
    rows = v.shape[0]
    if by % 8 == 0:
        return jnp.concatenate([v[by:], jnp.zeros((by, v.shape[1]), F32)], axis=0)
    return jnp.where(row_ids(v.shape) < rows - by, pltpu.roll(v, rows - by, 0), 0.0)


def vmem_call(body, out_shape, scratch=(), in_specs=None, remote=None):
    params = dict(vmem_limit_bytes=LIMIT)
    if remote is not None:
        params.update(collective_id=remote, has_side_effects=True)
    return pl.pallas_call(
        body,
        out_shape=out_shape,
        in_specs=in_specs,
        out_specs=jax.tree.map(lambda _: pl.BlockSpec(memory_space=VMEM), out_shape),
        scratch_shapes=list(scratch),
        compiler_params=pltpu.CompilerParams(**params),
    )


def in_vmem(count):
    return [pl.BlockSpec(memory_space=VMEM)] * count


def shaped(*shape):
    return jax.ShapeDtypeStruct(shape, F32)


def push_kernel(tele, flags, trans, sense, gain, masked, push, corr):
    rows, sensors = tele.shape
    segs, blocks = flags.shape
    seg_len, width = rows // segs, sensors // blocks
    spread = jnp.where(
        lax.broadcasted_iota(jnp.int32, (blocks, sensors), 1) // width
        == lax.broadcasted_iota(jnp.int32, (blocks, sensors), 0), 1.0, 0.0)
    wide = jnp.dot(flags[...], spread, preferred_element_type=F32)
    step = jnp.broadcast_to(wide[:, None, :], (segs, seg_len, sensors)).reshape(rows, sensors)
    values = tele[...] * step
    masked[...] = values
    push[...] = mm_nt(values, gain[...])
    moved = mm(sense[...], trans[...])
    for g in range(blocks):
        part = slice(g * width, (g + 1) * width)
        corr[g] = lax.dot_general(
            moved[part], gain[:, part], (((0,), (1,)), ((), ())),
            precision=lax.Precision.HIGHEST, preferred_element_type=F32)


def remote(src, dst, send, recv, where):
    return pltpu.make_async_remote_copy(
        src_ref=src, dst_ref=dst, send_sem=send, recv_sem=recv,
        device_id=where, device_id_type=MESH)


def pair_kernel(push, corr, flags, push_in, corr_in, flags_in, send, recv):
    tm, core = lax.axis_index("tm"), lax.axis_index("sens")
    other = (tm, 1 - core)
    barrier = pltpu.get_barrier_semaphore()
    pl.semaphore_signal(barrier, inc=1, device_id=other, device_id_type=MESH)
    pl.semaphore_wait(barrier, 1)
    half = push.shape[0] // 2
    theirs = pl.ds(pl.multiple_of((1 - core) * half, half), half)
    copies = [
        remote(corr, corr_in, send.at[0], recv.at[0], other),
        remote(push.at[theirs], push_in, send.at[1], recv.at[1], other),
        remote(flags, flags_in, send.at[2], recv.at[2], other),
    ]
    for copy in copies:
        copy.start()
    for copy in copies:
        copy.wait()


def maps_kernel(seg_len, push, push_in, corr, corr_in, flags, flags_in, trans,
                powers, ends, local, chunk, tree):
    core = lax.axis_index("sens")
    segs = ends.shape[0]
    width = trans.shape[0]
    blocks = corr.shape[0]
    levels = seg_len.bit_length() - 1

    def one(k):
        row = core * segs + k
        q = trans[...].T
        for g in range(blocks):
            q = q - flags[row, g] * corr[g] - flags_in[row, g] * corr_in[g]
        mine = pl.ds(pl.multiple_of(row * seg_len, seg_len), seg_len)
        here = pl.ds(pl.multiple_of(k * seg_len, seg_len), seg_len)
        v = push[mine] + push_in[here]
        for s in range(levels):
            powers[s, k] = q
            t = mm(jnp.concatenate([q, v], axis=0), q)
            v = v + shift_down(t[width:], 1 << s)
            q = t[:width]
        local[here] = v
        ends[k] = q
        tree[k, :width] = q
        tree[k, width:] = jnp.broadcast_to(v[seg_len - 1:], (8, width))

    unroll = 4

    def several(i, carry):
        for j in range(unroll):
            one(i * unroll + j)
        return carry

    lax.fori_loop(0, segs // unroll, several, 0)
    span = 1
    while span < segs:
        for k in range(0, segs, 2 * span):
            tree[k] = compose(tree[k], tree[k + span])
        span *= 2
    chunk[...] = tree[0]


def compose(first, second):
    width = second.shape[1]
    t = mm(first, second[:width])
    return jnp.concatenate([t[:width], t[width:] + second[width:]], axis=0)


def follow(x, step):
    width = step.shape[1]
    return mv(x, step[:width]) + step[width:]


def carry_kernel(n, chunk, start, entry, pair, chip, group, arrived, leaving, send, recv):
    tm, core = lax.axis_index("tm"), lax.axis_index("sens")
    place, mine = lax.rem(tm, GROUP), lax.div(tm, GROUP)
    groups = n // GROUP
    other = (tm, 1 - core)
    base = tm - place
    peers = [(base + lax.rem(place + k, GROUP), core) for k in range(1, GROUP)]
    barrier = pltpu.get_barrier_semaphore()
    chain = [(lax.rem(tm + by, n), core) for by in (GROUP, n - GROUP)]
    for peer in [other] + peers + chain:
        pl.semaphore_signal(barrier, inc=1, device_id=peer, device_id_type=MESH)
    pl.semaphore_wait(barrier, GROUP + 2)

    swap = remote(chunk, pair, send.at[0], recv.at[0], other)
    swap.start()
    swap.wait()
    own, their = chunk[...], pair[...]
    first = jnp.where(core == 0, own, their)
    chip[...] = compose(first, jnp.where(core == 0, their, own))
    copies = []
    for k, peer in enumerate(peers):
        copy = remote(chip, group.at[k], send.at[1 + k], recv.at[1 + k], peer)
        copy.start()
        copies.append(copy)
    for copy in copies:
        copy.wait()
    held = [chip[...]] + [group[k] for k in range(GROUP - 1)]
    ordered = []
    for p in range(GROUP):
        value = held[0]
        for k in range(1, GROUP):
            value = jnp.where(lax.rem(place - k + GROUP, GROUP) == p, held[k], value)
        ordered.append(value)
    low, high = compose(ordered[0], ordered[1]), compose(ordered[2], ordered[3])
    whole = compose(low, high)
    hand = remote(leaving, arrived, send.at[GROUP], recv.at[GROUP], (tm + GROUP, core))

    @pl.when(mine == 0)
    def _():
        arrived[...] = start[...]

    @pl.when(mine > 0)
    def _():
        remote(leaving, arrived, send.at[GROUP], recv.at[GROUP], (tm - GROUP, core)).wait_recv()

    x = arrived[...]
    leaving[...] = follow(x, whole)

    @pl.when(mine < groups - 1)
    def _():
        hand.start()

    x = jnp.where(place >= 2, follow(x, low), x)
    before = jnp.where(place >= 2, ordered[2], ordered[0])
    x = jnp.where(lax.rem(place, 2) == 1, follow(x, before), x)
    entry[...] = jnp.where(core == 1, follow(x, first), x)

    @pl.when(mine < groups - 1)
    def _():
        hand.wait_send()


def filter_kernel(n, seg_len, entry, powers, ends, local, trans, smooth,
                  drive_scan, gains, shift, final, states, filtered):
    levels, segs = powers.shape[:2]
    width = trans.shape[0]
    rows = segs * seg_len

    x = entry[...]
    for k in range(segs):
        states[k] = x
        x = mv(x, ends[k]) + local[(k + 1) * seg_len - 1:(k + 1) * seg_len]

    def one(k):
        here = pl.ds(pl.multiple_of(k * seg_len, seg_len), seg_len)
        w = jnp.concatenate([states[k]] * (seg_len // 8), axis=0)
        ids = row_ids(w.shape)
        for s in range(levels):
            w = jnp.where((ids // (1 << s)) % 2 == 1, mv(w, powers[s, k]), w)
        filtered[here] = local[here] + mv(w, powers[0, k])

    unroll = 4

    def several(i, carry):
        for j in range(unroll):
            one(i * unroll + j)
        return carry

    lax.fori_loop(0, segs // unroll, several, 0)
    f = filtered[...]
    ahead = mm_nt(f, trans[...])
    v = f - mm_nt(ahead, smooth[...])
    last = jnp.broadcast_to(ahead[rows - 1:], (8, width))
    final[...] = last
    p = smooth[...].T
    span, level = 1, 0
    while span < rows:
        gains[level] = p
        t = mm(jnp.concatenate([p, v], axis=0), p)
        v = v + shift_up(t[width:], span)
        p = t[:width]
        span, level = span * 2, level + 1
    gains[level] = p
    drive_scan[...] = v
    is_last = (lax.axis_index("tm") == n - 1) & (lax.axis_index("sens") == 1)
    s = jnp.broadcast_to(v[:1], (8, width))
    shift[...] = jnp.where(is_last, s + mm(last, p), s)


def smooth_kernel(n, drive_scan, gains, shift, final, out, entry, shifts, send, recv):
    tm, core = lax.axis_index("tm"), lax.axis_index("sens")
    chunks = 2 * n
    me = tm * 2 + core
    half, width = drive_scan.shape
    barrier = pltpu.get_barrier_semaphore()

    def place(k):
        c = lax.rem(me + k, chunks)
        return (lax.div(c, 2), lax.rem(c, 2))

    def greet(k, carry):
        pl.semaphore_signal(barrier, inc=1, device_id=place(k), device_id_type=MESH)
        return carry

    lax.fori_loop(1, chunks, greet, 0)
    pl.semaphore_wait(barrier, chunks - 1)

    def launch(k, carry):
        remote(shift, shifts.at[me], send.at[k], recv.at[me], place(k)).start()
        return carry

    lax.fori_loop(1, chunks, launch, 0)
    shifts[me] = shift[...]

    def land(k, carry):
        c = lax.rem(me + k, chunks)
        remote(shift, shifts.at[c], send.at[k], recv.at[c], place(k)).wait()
        return carry

    lax.fori_loop(1, chunks, land, 0)
    v = shifts[:, 0, :]
    levels = gains.shape[0] - 1
    p = gains[levels]
    span = 1
    while span < chunks:
        t = mm(jnp.concatenate([p, v], axis=0), p)
        v = v + shift_up(t[width:], span)
        p = t[:width]
        span *= 2
    x = jnp.sum(jnp.where(row_ids(v.shape) == me + 1, v, 0.0), axis=0, keepdims=True)
    x = jnp.where(me == chunks - 1, final[...], jnp.broadcast_to(x, (8, width)))
    after = jnp.where(row_ids(v.shape) == 2 * tm + 2, v, 0.0)
    entry[...] = jnp.broadcast_to(jnp.sum(after, axis=0, keepdims=True), (8, width))
    w = x
    ids = 7 - row_ids(w.shape)
    for s in range(3):
        w = jnp.where((ids // (1 << s)) % 2 == 1, mv(w, gains[s]), w)
    w = mv(w, gains[0])
    for s in range(3, levels):
        w = jnp.concatenate([mv(w, gains[s]), w], axis=0)
    mine = pl.ds(pl.multiple_of(core * half, half), half)
    out[mine] = drive_scan[...] + w
    swap = remote(out.at[mine], out.at[mine], send.at[0], recv.at[chunks], (tm, 1 - core))
    swap.start()
    swap.wait()


def stats_kernel(n, smoothed, entry, masked, flags, stats):
    rows, width = smoothed.shape
    segs, blocks = flags.shape
    seg_len = rows // segs
    sensors = masked.shape[1]
    tm, core = lax.axis_index("tm"), lax.axis_index("sens")
    x = smoothed[...]
    ids = row_ids((rows, width))
    weight = jnp.where((tm == n - 1) & (ids == rows - 1), 0.0, 1.0)
    prior = x * weight
    above = pltpu.roll(x, rows - 1, 0)
    above = jnp.where(ids == rows - 1, jnp.broadcast_to(entry[:1], (rows, width)), above)
    size = sensors // blocks
    cross = mm_tn(masked[...], x)
    stats[:width] = mm_tn(prior, x)
    stats[width:2 * width] = mm_tn(above, prior)
    for g in range(blocks):
        column = jnp.broadcast_to(flags[:, g:g + 1], (segs, width))
        step = jnp.broadcast_to(column[:, None, :], (segs, seg_len, width)).reshape(rows, width)
        at = 2 * width + g * (width + size)
        stats[at:at + width] = mm_tn(x * step, x)
        stats[at + width:at + width + size] = cross[g * size:(g + 1) * size]


def sum_kernel(n, count, size, stats, system, parts, total, send, recv, send2, recv2):
    me, core = lax.axis_index("tm"), lax.axis_index("sens")
    width = stats.shape[1]
    piece = stats.shape[0] // n
    first, later = 2 * width // piece, (width + size) // piece
    apart = n // count
    barrier = pltpu.get_barrier_semaphore()
    system[...] = jnp.zeros_like(system)

    def at(c):
        return pl.ds(pl.multiple_of(c * piece, piece), piece)

    def peer(k):
        return lax.rem(me + k, n)

    def greet(k, carry):
        pl.semaphore_signal(barrier, inc=1, device_id=(peer(k), core), device_id_type=MESH)
        return carry

    lax.fori_loop(1, n, greet, 0)
    pl.semaphore_wait(barrier, n - 1)

    def scatter(k, carry):
        c = peer(k)
        remote(stats.at[at(c)], parts.at[me], send.at[k], recv.at[me], (c, core)).start()
        return carry

    lax.fori_loop(1, n, scatter, 0)
    parts[me] = stats[at(me)]

    def land(k, carry):
        c = peer(k)
        remote(stats.at[at(c)], parts.at[c], send.at[k], recv.at[c], (c, core)).wait()
        return carry

    lax.fori_loop(1, n, land, 0)
    total[...] = jnp.sum(parts[...], axis=0)
    past = jnp.maximum(me - first, 0)
    which = jnp.where(me < first, 0, 1 + past // later)
    slot = jnp.where(me < first, me, past % later)
    owner = which * apart
    hand = remote(total, system.at[at(slot)], send2.at[0], recv2.at[slot], (owner, core))

    @pl.when(owner == me)
    def _():
        system[at(slot)] = total[...]

    @pl.when(owner != me)
    def _():
        hand.start()

    task = me // apart

    @pl.when((task * apart == me) & (task < count))
    def _():
        begin = jnp.where(task == 0, 0, first + (task - 1) * later)

        def take(j, carry):
            @pl.when(begin + j != me)
            def _():
                remote(total, system.at[at(j)], send2.at[0], recv2.at[j], (peer(1), core)).wait_recv()
            return carry

        lax.fori_loop(0, jnp.where(task == 0, first, later), take, 0)

    @pl.when(owner != me)
    def _():
        hand.wait_send()


def share_kernel(n, count, size, solved, new_transition, new_sensing, send, recv):
    me, core = lax.axis_index("tm"), lax.axis_index("sens")
    apart = n // count
    barrier = pltpu.get_barrier_semaphore()

    def peer(k):
        return (lax.rem(me + k, n), core)

    def greet(k, carry):
        pl.semaphore_signal(barrier, inc=1, device_id=peer(k), device_id_type=MESH)
        return carry

    lax.fori_loop(1, n, greet, 0)
    pl.semaphore_wait(barrier, n - 1)
    for s in range(count):
        rows = pl.ds((s - 1) * size, size)
        source = solved if s == 0 else solved.at[pl.ds(0, size)]
        target = new_transition if s == 0 else new_sensing.at[rows]

        def copy(k):
            return remote(source, target, send.at[k], recv.at[s], peer(k))

        @pl.when(me == s * apart)
        def _():
            def launch(k, carry):
                copy(k).start()
                return carry

            lax.fori_loop(1, n, launch, 0)
            if s == 0:
                new_transition[...] = solved[...]
            else:
                new_sensing[rows] = solved[:size]

    for s in range(count):
        rows = pl.ds((s - 1) * size, size)
        source = solved if s == 0 else solved.at[pl.ds(0, size)]
        target = new_transition if s == 0 else new_sensing.at[rows]

        def copy(k):
            return remote(source, target, send.at[k], recv.at[s], peer(k))

        @pl.when(me == s * apart)
        def _():
            def close(k, carry):
                copy(k).wait_send()
                return carry

            lax.fori_loop(1, n, close, 0)

        @pl.when(me != s * apart)
        def _():
            copy(1).wait_recv()


def inverse_factor(a):
    size = a.shape[0]
    shape = (size, 2 * size)
    rows = row_ids(shape)
    cols = lax.broadcasted_iota(jnp.int32, shape, 1)
    a = jnp.concatenate([a, jnp.where(rows + size == cols, 1.0, 0.0)[:, size:]], axis=1)
    scale = jnp.zeros((size, size), F32)
    for k in range(size):
        inv = 1.0 / a[k:k + 1, k:k + 1]
        scale = jnp.where(rows[:, :size] == k, inv, scale)
        c = jnp.where(rows > k, a[:, k:k + 1], 0.0) * inv
        a = a - c * a[k:k + 1]
    return a[:, size:] * jnp.sqrt(scale)


def solve_kernel(ridge, system, solved, work):
    width = system.shape[1]
    eye = jnp.where(
        row_ids((width, width)) == lax.broadcasted_iota(jnp.int32, (width, width), 1), ridge, 0.0)
    work[:, :width] = system[:width] + eye
    work[:, width:] = system[width:].T
    steps = width // PIVOT
    inverses = []
    for j in range(steps):
        lo, hi = j * PIVOT, (j + 1) * PIVOT
        inv = inverse_factor(work[lo:hi, lo:hi])
        inverses.append(inv)
        row = mm(inv, work[lo:hi, :])
        work[lo:hi, :] = row
        if hi < width:
            work[hi:, :] = work[hi:, :] - mm_tn(row[:, hi:width], row)
    x = None
    for j in reversed(range(steps)):
        lo, hi = j * PIVOT, (j + 1) * PIVOT
        rhs = work[lo:hi, width:]
        if x is not None:
            rhs = rhs - mm(work[lo:hi, hi:width], x)
        piece = mm_tn(inverses[j], rhs)
        x = piece if x is None else jnp.concatenate([piece, x], axis=0)
    solved[...] = x.T


def on_device(n, telemetry, present, transition, sensing, filter_gain, smooth_gain, initial_state):
    width = transition.shape[0]
    rows, sensors = telemetry.shape
    segs, blocks = present.shape
    seg_len = rows // segs
    half, half_segs = rows // 2, segs // 2
    dma = pltpu.SemaphoreType.DMA
    flags = present.astype(F32)
    wide_flags = jnp.pad(flags, ((0, 0), (0, 128 - blocks)))
    start = jnp.broadcast_to(initial_state[None], (8, width))

    masked, push, corr = vmem_call(
        push_kernel,
        (shaped(rows, sensors), shaped(rows, width), shaped(blocks, width, width)),
        in_specs=in_vmem(5),
    )(telemetry, flags, transition, sensing, filter_gain)
    push_in, corr_in, flags_in = vmem_call(
        pair_kernel,
        (shaped(half, width), shaped(blocks, width, width), shaped(segs, 128)),
        [dma((3,)), dma((3,))],
        in_vmem(3), remote=1,
    )(push, corr, wide_flags)
    levels = seg_len.bit_length() - 1
    scalars = pl.BlockSpec(memory_space=pltpu.SMEM)
    powers, ends, local, chunk = vmem_call(
        functools.partial(maps_kernel, seg_len),
        (shaped(levels, half_segs, width, width), shaped(half_segs, width, width),
         shaped(half, width), shaped(width + 8, width)),
        [VMEM((half_segs, width + 8, width), F32)],
        in_vmem(4) + [scalars, scalars] + in_vmem(1),
    )(push, push_in, corr, corr_in, wide_flags, flags_in, transition)
    entry = vmem_call(
        functools.partial(carry_kernel, n),
        shaped(8, width),
        [VMEM((width + 8, width), F32), VMEM((width + 8, width), F32),
         VMEM((GROUP - 1, width + 8, width), F32), VMEM((8, width), F32), VMEM((8, width), F32),
         dma((GROUP + 1,)), dma((GROUP + 1,))],
        in_vmem(2), remote=2,
    )(chunk, start)
    back_levels = half.bit_length() - 1
    drive_scan, gains, shift, final = vmem_call(
        functools.partial(filter_kernel, n, seg_len),
        (shaped(half, width), shaped(back_levels + 1, width, width), shaped(8, width),
         shaped(8, width)),
        [VMEM((half_segs, 8, width), F32), VMEM((half, width), F32)],
        in_vmem(6),
    )(entry, powers, ends, local, transition, smooth_gain)
    smoothed, entry_back = vmem_call(
        functools.partial(smooth_kernel, n),
        (shaped(rows, width), shaped(8, width)),
        [VMEM((2 * n, 8, width), F32), dma((2 * n,)), dma((2 * n + 1,))],
        in_vmem(4), remote=3,
    )(drive_scan, gains, shift, final)
    stats = vmem_call(
        functools.partial(stats_kernel, n),
        shaped((blocks + 2) * width + sensors, width),
        in_specs=in_vmem(4),
    )(smoothed, entry_back, masked, flags)
    count, size = blocks + 1, sensors // blocks
    piece = stats.shape[0] // n
    system = vmem_call(
        functools.partial(sum_kernel, n, count, size),
        shaped(2 * width, width),
        [VMEM((n, piece, width), F32), VMEM((piece, width), F32),
         dma((n,)), dma((n,)), dma((1,)), dma((2 * width // piece,))],
        in_vmem(1), remote=4,
    )(stats)
    solved = vmem_call(
        functools.partial(solve_kernel, RIDGE * rows * n),
        shaped(width, width),
        [VMEM((width, 2 * width), F32)],
        in_vmem(1),
    )(system)
    new_transition, new_sensing = vmem_call(
        functools.partial(share_kernel, n, count, size),
        (shaped(width, width), shaped(sensors, width)),
        [dma((n,)), dma((count,))],
        in_vmem(1), remote=5,
    )(solved)
    return (new_transition, new_sensing, smoothed)


def solution(mesh):
    placed = (P("tm", "sens"), P("tm", "sens"), P(), P("sens", None), P(None, "sens"), P(), P())
    return jax.shard_map(
        functools.partial(on_device, mesh.shape["tm"]),
        mesh=mesh,
        in_specs=placed,
        out_specs=(P(), P("sens", None), P("tm", None)),
        check_vma=False,
    )
```

```python
import functools

import jax
import jax.numpy as jnp
from jax import lax
from jax.experimental import pallas as pl
from jax.experimental.pallas import tpu as pltpu
from jax.sharding import PartitionSpec as P

RIDGE = 0.001
GROUP = 4
PIVOT = 32
TOGETHER = 4
REDUCERS = 16
MESH = pl.DeviceIdType.MESH
VMEM = pltpu.VMEM
F32 = jnp.float32
LIMIT = 48 * 1024 * 1024


def mm(a, b):
    return jnp.dot(a, b, precision=lax.Precision.HIGHEST, preferred_element_type=F32)


def mv(a, b):
    return jnp.dot(a, b, precision=lax.Precision.HIGH, preferred_element_type=F32)


def mm_tn(a, b):
    return lax.dot_general(
        a, b, (((0,), (0,)), ((), ())),
        precision=lax.Precision.HIGHEST, preferred_element_type=F32,
    )


def mm_nt(a, b):
    return lax.dot_general(
        a, b, (((1,), (1,)), ((), ())),
        precision=lax.Precision.HIGHEST, preferred_element_type=F32,
    )


def row_ids(shape):
    return lax.broadcasted_iota(jnp.int32, shape, 0)


def shift_down(v, by):
    if by % 8 == 0:
        return jnp.concatenate([jnp.zeros((by, v.shape[1]), F32), v[:-by]], axis=0)
    return jnp.where(row_ids(v.shape) >= by, pltpu.roll(v, by, 0), 0.0)


def shift_up(v, by):
    rows = v.shape[0]
    if by % 8 == 0:
        return jnp.concatenate([v[by:], jnp.zeros((by, v.shape[1]), F32)], axis=0)
    return jnp.where(row_ids(v.shape) < rows - by, pltpu.roll(v, rows - by, 0), 0.0)


def vmem_call(body, out_shape, scratch=(), in_specs=None, remote=None):
    params = dict(vmem_limit_bytes=LIMIT)
    if remote is not None:
        params.update(collective_id=remote, has_side_effects=True)
    return pl.pallas_call(
        body,
        out_shape=out_shape,
        in_specs=in_specs,
        out_specs=jax.tree.map(lambda _: pl.BlockSpec(memory_space=VMEM), out_shape),
        scratch_shapes=list(scratch),
        compiler_params=pltpu.CompilerParams(**params),
    )


def in_vmem(count):
    return [pl.BlockSpec(memory_space=VMEM)] * count


def shaped(*shape):
    return jax.ShapeDtypeStruct(shape, F32)


def push_kernel(tele, flags, trans, sense, gain, masked, push, corr):
    rows, sensors = tele.shape
    segs, blocks = flags.shape
    seg_len, width = rows // segs, sensors // blocks
    spread = jnp.where(
        lax.broadcasted_iota(jnp.int32, (blocks, sensors), 1) // width
        == lax.broadcasted_iota(jnp.int32, (blocks, sensors), 0), 1.0, 0.0)
    wide = jnp.dot(flags[...], spread, preferred_element_type=F32)
    step = jnp.broadcast_to(wide[:, None, :], (segs, seg_len, sensors)).reshape(rows, sensors)
    values = tele[...] * step
    masked[...] = values
    push[...] = mm_nt(values, gain[...])
    moved = mm(sense[...], trans[...])
    for g in range(blocks):
        part = slice(g * width, (g + 1) * width)
        corr[g] = lax.dot_general(
            moved[part], gain[:, part], (((0,), (1,)), ((), ())),
            precision=lax.Precision.HIGHEST, preferred_element_type=F32)


def remote(src, dst, send, recv, where):
    return pltpu.make_async_remote_copy(
        src_ref=src, dst_ref=dst, send_sem=send, recv_sem=recv,
        device_id=where, device_id_type=MESH)


def pair_kernel(push, corr, flags, push_in, corr_in, flags_in, send, recv):
    tm, core = lax.axis_index("tm"), lax.axis_index("sens")
    other = (tm, 1 - core)
    barrier = pltpu.get_barrier_semaphore()
    pl.semaphore_signal(barrier, inc=1, device_id=other, device_id_type=MESH)
    pl.semaphore_wait(barrier, 1)
    half = push.shape[0] // 2
    theirs = pl.ds(pl.multiple_of((1 - core) * half, half), half)
    copies = [
        remote(corr, corr_in, send.at[0], recv.at[0], other),
        remote(push.at[theirs], push_in, send.at[1], recv.at[1], other),
        remote(flags, flags_in, send.at[2], recv.at[2], other),
    ]
    for copy in copies:
        copy.start()
    for copy in copies:
        copy.wait()


def maps_kernel(seg_len, push, push_in, corr, corr_in, flags, flags_in, trans,
                powers, ends, local, chunk, tree):
    core = lax.axis_index("sens")
    segs = ends.shape[0]
    width = trans.shape[0]
    blocks = corr.shape[0]
    levels = seg_len.bit_length() - 1

    def one(k):
        row = core * segs + k
        q = trans[...].T
        for g in range(blocks):
            q = q - flags[row, g] * corr[g] - flags_in[row, g] * corr_in[g]
        mine = pl.ds(pl.multiple_of(row * seg_len, seg_len), seg_len)
        here = pl.ds(pl.multiple_of(k * seg_len, seg_len), seg_len)
        v = push[mine] + push_in[here]
        for s in range(levels):
            powers[s, k] = q
            t = mm(jnp.concatenate([q, v], axis=0), q)
            v = v + shift_down(t[width:], 1 << s)
            q = t[:width]
        local[here] = v
        ends[k] = q
        tree[k, :width] = q
        tree[k, width:] = jnp.broadcast_to(v[seg_len - 1:], (8, width))

    unroll = 4

    def several(i, carry):
        for j in range(unroll):
            one(i * unroll + j)
        return carry

    lax.fori_loop(0, segs // unroll, several, 0)
    span = 1
    while span < segs:
        for k in range(0, segs, 2 * span):
            tree[k] = compose(tree[k], tree[k + span])
        span *= 2
    chunk[...] = tree[0]


def compose(first, second):
    width = second.shape[1]
    t = mm(first, second[:width])
    return jnp.concatenate([t[:width], t[width:] + second[width:]], axis=0)


def follow(x, step):
    width = step.shape[1]
    return mv(x, step[:width]) + step[width:]


def carry_kernel(n, chunk, start, entry, pair, chip, group, arrived, leaving, send, recv):
    tm, core = lax.axis_index("tm"), lax.axis_index("sens")
    place, mine = lax.rem(tm, GROUP), lax.div(tm, GROUP)
    groups = n // GROUP
    other = (tm, 1 - core)
    base = tm - place
    peers = [(base + lax.rem(place + k, GROUP), core) for k in range(1, GROUP)]
    barrier = pltpu.get_barrier_semaphore()
    chain = [(lax.rem(tm + by, n), core) for by in (GROUP, n - GROUP)]
    for peer in [other] + peers + chain:
        pl.semaphore_signal(barrier, inc=1, device_id=peer, device_id_type=MESH)
    pl.semaphore_wait(barrier, GROUP + 2)

    swap = remote(chunk, pair, send.at[0], recv.at[0], other)
    swap.start()
    swap.wait()
    own, their = chunk[...], pair[...]
    first = jnp.where(core == 0, own, their)
    chip[...] = compose(first, jnp.where(core == 0, their, own))
    copies = []
    for k, peer in enumerate(peers):
        copy = remote(chip, group.at[k], send.at[1 + k], recv.at[1 + k], peer)
        copy.start()
        copies.append(copy)
    for copy in copies:
        copy.wait()
    held = [chip[...]] + [group[k] for k in range(GROUP - 1)]
    ordered = []
    for p in range(GROUP):
        value = held[0]
        for k in range(1, GROUP):
            value = jnp.where(lax.rem(place - k + GROUP, GROUP) == p, held[k], value)
        ordered.append(value)
    low, high = compose(ordered[0], ordered[1]), compose(ordered[2], ordered[3])
    whole = compose(low, high)
    hand = remote(leaving, arrived, send.at[GROUP], recv.at[GROUP], (tm + GROUP, core))

    @pl.when(mine == 0)
    def _():
        arrived[...] = start[...]

    @pl.when(mine > 0)
    def _():
        remote(leaving, arrived, send.at[GROUP], recv.at[GROUP], (tm - GROUP, core)).wait_recv()

    x = arrived[...]
    leaving[...] = follow(x, whole)

    @pl.when(mine < groups - 1)
    def _():
        hand.start()

    x = jnp.where(place >= 2, follow(x, low), x)
    before = jnp.where(place >= 2, ordered[2], ordered[0])
    x = jnp.where(lax.rem(place, 2) == 1, follow(x, before), x)
    entry[...] = jnp.where(core == 1, follow(x, first), x)

    @pl.when(mine < groups - 1)
    def _():
        hand.wait_send()


def filter_kernel(n, seg_len, entry, powers, ends, local, trans, smooth,
                  drive_scan, gains, shift, final, states, filtered):
    levels, segs = powers.shape[:2]
    width = trans.shape[0]
    rows = segs * seg_len

    x = entry[...]
    for k in range(segs):
        states[k] = x
        x = mv(x, ends[k]) + local[(k + 1) * seg_len - 1:(k + 1) * seg_len]

    def one(k):
        here = pl.ds(pl.multiple_of(k * seg_len, seg_len), seg_len)
        w = jnp.concatenate([states[k]] * (seg_len // 8), axis=0)
        ids = row_ids(w.shape)
        for s in range(levels):
            w = jnp.where((ids // (1 << s)) % 2 == 1, mv(w, powers[s, k]), w)
        filtered[here] = local[here] + mv(w, powers[0, k])

    unroll = 4

    def several(i, carry):
        for j in range(unroll):
            one(i * unroll + j)
        return carry

    lax.fori_loop(0, segs // unroll, several, 0)
    f = filtered[...]
    ahead = mm_nt(f, trans[...])
    v = f - mm_nt(ahead, smooth[...])
    last = jnp.broadcast_to(ahead[rows - 1:], (8, width))
    final[...] = last
    p = smooth[...].T
    span, level = 1, 0
    while span < rows:
        gains[level] = p
        t = mm(jnp.concatenate([p, v], axis=0), p)
        v = v + shift_up(t[width:], span)
        p = t[:width]
        span, level = span * 2, level + 1
    gains[level] = p
    drive_scan[...] = v
    is_last = (lax.axis_index("tm") == n - 1) & (lax.axis_index("sens") == 1)
    s = jnp.broadcast_to(v[:1], (8, width))
    shift[...] = jnp.where(is_last, s + mm(last, p), s)


def smooth_kernel(n, drive_scan, gains, shift, final, out, entry, shifts, send, recv):
    tm, core = lax.axis_index("tm"), lax.axis_index("sens")
    chunks = 2 * n
    me = tm * 2 + core
    half, width = drive_scan.shape
    barrier = pltpu.get_barrier_semaphore()

    def place(k):
        c = lax.rem(me + k, chunks)
        return (lax.div(c, 2), lax.rem(c, 2))

    def greet(k, carry):
        pl.semaphore_signal(barrier, inc=1, device_id=place(k), device_id_type=MESH)
        return carry

    lax.fori_loop(1, chunks, greet, 0)
    pl.semaphore_wait(barrier, chunks - 1)

    def launch(k, carry):
        remote(shift, shifts.at[me], send.at[k], recv.at[me], place(k)).start()
        return carry

    lax.fori_loop(1, chunks, launch, 0)
    shifts[me] = shift[...]

    def land(k, carry):
        c = lax.rem(me + k, chunks)
        remote(shift, shifts.at[c], send.at[k], recv.at[c], place(k)).wait()
        return carry

    lax.fori_loop(1, chunks, land, 0)
    v = shifts[:, 0, :]
    levels = gains.shape[0] - 1
    p = gains[levels]
    span = 1
    while span < chunks:
        t = mm(jnp.concatenate([p, v], axis=0), p)
        v = v + shift_up(t[width:], span)
        p = t[:width]
        span *= 2
    x = jnp.sum(jnp.where(row_ids(v.shape) == me + 1, v, 0.0), axis=0, keepdims=True)
    x = jnp.where(me == chunks - 1, final[...], jnp.broadcast_to(x, (8, width)))
    after = jnp.where(row_ids(v.shape) == 2 * tm + 2, v, 0.0)
    entry[...] = jnp.broadcast_to(jnp.sum(after, axis=0, keepdims=True), (8, width))
    w = x
    ids = 7 - row_ids(w.shape)
    for s in range(3):
        w = jnp.where((ids // (1 << s)) % 2 == 1, mv(w, gains[s]), w)
    w = mv(w, gains[0])
    for s in range(3, levels):
        w = jnp.concatenate([mv(w, gains[s]), w], axis=0)
    mine = pl.ds(pl.multiple_of(core * half, half), half)
    out[mine] = drive_scan[...] + w
    swap = remote(out.at[mine], out.at[mine], send.at[0], recv.at[chunks], (tm, 1 - core))
    swap.start()
    swap.wait()


def stats_kernel(n, reducers, smoothed, entry, masked, flags, stats, smoothed_out):
    rows, width = smoothed.shape
    segs, blocks = flags.shape
    seg_len = rows // segs
    sensors = masked.shape[1]
    tm, core = lax.axis_index("tm"), lax.axis_index("sens")
    x = smoothed[...]
    ids = row_ids((rows, width))
    weight = jnp.where((tm == n - 1) & (ids == rows - 1), 0.0, 1.0)
    prior = x * weight
    above = pltpu.roll(x, rows - 1, 0)
    above = jnp.where(ids == rows - 1, jnp.broadcast_to(entry[:1], (rows, width)), above)
    size = sensors // blocks
    cross = mm_tn(masked[...], x)
    smoothed_out[...] = x
    lag = jnp.concatenate([mm_tn(prior, x), mm_tn(above, prior)], axis=0)
    held = []
    for g in range(blocks):
        column = jnp.broadcast_to(flags[:, g:g + 1], (segs, width))
        step = jnp.broadcast_to(column[:, None, :], (segs, seg_len, width)).reshape(rows, width)
        held += [mm_tn(x * step, x), cross[g * size:(g + 1) * size]]
    sensor = jnp.concatenate(held, axis=0)
    lag_piece, piece = lag.shape[0] // reducers, sensor.shape[0] // reducers
    for r in range(reducers):
        at = r * (lag_piece + piece)
        stats[at:at + lag_piece] = lag[r * lag_piece:(r + 1) * lag_piece]
        stats[at + lag_piece:at + lag_piece + piece] = sensor[r * piece:(r + 1) * piece]


def sum_kernel(n, reducers, blocks, stats, lag, system, parts, total,
               send, recv, send2, recv2, send3, recv3):
    me, core = lax.axis_index("tm"), lax.axis_index("sens")
    step = n // reducers
    mine, reduces = me // step, me % step == 0
    lag_piece, piece = lag.shape[0] // reducers, system.shape[0] * blocks // reducers
    per_system = reducers // blocks
    groups = n // blocks
    both = lag_piece + piece
    barrier = pltpu.get_barrier_semaphore()

    def peer(k):
        return lax.rem(me + k, n)

    def greet(k, carry):
        pl.semaphore_signal(barrier, inc=1, device_id=(peer(k), core), device_id_type=MESH)
        return carry

    lax.fori_loop(1, n, greet, 0)
    pl.semaphore_wait(barrier, n - 1)

    def part_of(c):
        return stats.at[pl.ds(pl.multiple_of(c * both, both), both)]

    def give(k):
        c = lax.rem(mine + k, reducers)
        return remote(part_of(c), parts.at[me], send.at[k], recv.at[me], (c * step, core))

    def scatter(k, carry):
        give(k).start()
        return carry

    def sent(k, carry):
        give(k).wait_send()
        return carry

    def land(k, carry):
        c = peer(k)
        remote(part_of(0), parts.at[c], send.at[0], recv.at[c], (c, core)).wait_recv()
        return carry

    lax.fori_loop(1, reducers, scatter, 0)
    if step > 1:
        @pl.when(me % step != 0)
        def _():
            give(0).start()

    task, slot = mine // per_system, mine % per_system
    lag_at = pl.ds(pl.multiple_of(mine * lag_piece, lag_piece), lag_piece)
    system_at = pl.ds(pl.multiple_of(slot * piece, piece), piece)
    lag_part, system_part = total.at[pl.ds(0, lag_piece)], total.at[pl.ds(lag_piece, piece)]

    def tell(k):
        return remote(lag_part, lag.at[lag_at], send2.at[k], recv2.at[mine], (peer(k), core))

    def place(g):
        return lax.rem(me // blocks + g, groups) * blocks + task

    def hand(g):
        return remote(system_part, system.at[system_at], send3.at[g], recv3.at[slot], (place(g), core))

    @pl.when(reduces)
    def _():
        lax.fori_loop(1, n, land, 0)
        parts[me] = part_of(mine)[...]
        total[...] = jnp.sum(parts[...], axis=0)
        lag[lag_at] = total[:lag_piece]

        def spread(g, carry):
            @pl.when(place(g) != me)
            def _():
                hand(g).start()
            return carry

        lax.fori_loop(0, groups, spread, 0)

        @pl.when(me % blocks == task)
        def _():
            system[system_at] = total[lag_piece:]

        def announce(k, carry):
            tell(k).start()
            return carry

        lax.fori_loop(1, n, announce, 0)

    def take(j, carry):
        @pl.when((me % blocks * per_system + j) * step != me)
        def _():
            remote(system_part, system.at[pl.ds(pl.multiple_of(j * piece, piece), piece)],
                   send3.at[0], recv3.at[j], (peer(1), core)).wait_recv()
        return carry

    lax.fori_loop(0, per_system, take, 0)

    def hear(r, carry):
        @pl.when(r * step != me)
        def _():
            remote(lag_part, lag.at[pl.ds(pl.multiple_of(r * lag_piece, lag_piece), lag_piece)],
                   send2.at[0], recv2.at[r], (peer(1), core)).wait_recv()
        return carry

    lax.fori_loop(0, reducers, hear, 0)
    lax.fori_loop(1, reducers, sent, 0)
    if step > 1:
        @pl.when(me % step != 0)
        def _():
            give(0).wait_send()

    @pl.when(reduces)
    def _():
        def told(k, carry):
            tell(k).wait_send()
            return carry

        def handed(g, carry):
            @pl.when(place(g) != me)
            def _():
                hand(g).wait_send()
            return carry

        lax.fori_loop(1, n, told, 0)
        lax.fori_loop(0, groups, handed, 0)


def share_kernel(blocks, solved, new_sensing, send, recv):
    me, core = lax.axis_index("tm"), lax.axis_index("sens")
    size = solved.shape[0]
    task = lax.rem(me, blocks)
    base = me - task
    barrier = pltpu.get_barrier_semaphore()
    peers = [(base + lax.rem(task + k, blocks), core) for k in range(1, blocks)]
    for peer in peers:
        pl.semaphore_signal(barrier, inc=1, device_id=peer, device_id_type=MESH)
    pl.semaphore_wait(barrier, blocks - 1)

    def at(t):
        return pl.ds(pl.multiple_of(t * size, size), size)

    for k, peer in enumerate(peers):
        remote(solved, new_sensing.at[at(task)], send.at[k], recv.at[k], peer).start()
    new_sensing[at(task)] = solved[...]
    for k, peer in enumerate(peers):
        source = lax.rem(task - k - 1 + blocks, blocks)
        remote(solved, new_sensing.at[at(source)], send.at[k], recv.at[k], peer).wait()


def inverse_factor(a):
    count, size = a.shape[:2]
    shape = (count, size, 2 * size)
    wide = (count, 1, 2 * size)
    rows = lax.broadcasted_iota(jnp.int32, shape, 1)
    cols = lax.broadcasted_iota(jnp.int32, shape, 2)
    a = jnp.concatenate([a, jnp.where(rows + size == cols, 1.0, 0.0)[:, :, size:]], axis=2)
    scale = jnp.zeros(shape, F32)
    for k in range(0, size, TOGETHER):
        own = range(TOGETHER)
        pivot = [[jnp.broadcast_to(a[:, k + i:k + i + 1, k + j:k + j + 1], wide) if j >= i else None
                  for j in own] for i in own]
        r = [a[:, k + i:k + i + 1, :] for i in own]
        c = [jnp.broadcast_to(a[:, :, k + i:k + i + 1], shape) for i in own]
        for i in own:
            inv = 1.0 / pivot[i][i]
            scale = jnp.where(rows == k + i, inv, scale)
            for j in range(i + 1, TOGETHER):
                m = pivot[i][j] * inv
                for l in range(j, TOGETHER):
                    pivot[j][l] = pivot[j][l] - m * pivot[i][l]
                r[j] = r[j] - m * r[i]
                c[j] = c[j] - m * c[i]
            a = a - jnp.where(rows > k + i, c[i] * inv, 0.0) * r[i]
    return (a * jnp.sqrt(scale))[:, :, size:]


def solve_kernel(ridge, lag, system, new_transition, solved):
    width = lag.shape[1]
    size = solved.shape[0]
    eye = jnp.where(
        row_ids((width, width)) == lax.broadcasted_iota(jnp.int32, (width, width), 1), ridge, 0.0)
    left = system[width:].T
    left = jnp.concatenate([left] * (width // size), axis=1)
    rest = [jnp.concatenate([lag[:width] + eye, lag[width:].T], axis=1),
            jnp.concatenate([system[:width] + eye, left], axis=1)]
    both = range(2)
    steps = width // PIVOT
    inverses, panels = [], []
    for j in range(steps):
        lo, hi = j * PIVOT, (j + 1) * PIVOT
        inv = inverse_factor(jnp.stack([rest[s][:PIVOT, lo:hi] for s in both]))
        panel = [mm(inv[s], rest[s][:PIVOT]) for s in both]
        inverses.append(inv)
        panels.append(panel)
        if hi < width:
            rest = [rest[s][PIVOT:] - mm_tn(panel[s][:, :width], panel[s])[hi:] for s in both]
    x = [None, None]
    for j in reversed(range(steps)):
        hi = (j + 1) * PIVOT
        for s in both:
            rhs = panels[j][s][:, width:]
            if x[s] is not None:
                full = jnp.concatenate([jnp.zeros((hi, width), F32), x[s]], axis=0)
                rhs = rhs - mm(panels[j][s][:, :width], full)
            piece = mm_tn(inverses[j][s], rhs)
            x[s] = piece if x[s] is None else jnp.concatenate([piece, x[s]], axis=0)
    new_transition[...] = x[0].T
    solved[...] = x[1].T[:size]


def on_device(n, telemetry, present, transition, sensing, filter_gain, smooth_gain, initial_state):
    width = transition.shape[0]
    rows, sensors = telemetry.shape
    segs, blocks = present.shape
    seg_len = rows // segs
    half, half_segs = rows // 2, segs // 2
    dma = pltpu.SemaphoreType.DMA
    flags = present.astype(F32)
    wide_flags = jnp.pad(flags, ((0, 0), (0, 128 - blocks)))
    start = jnp.broadcast_to(initial_state[None], (8, width))

    masked, push, corr = vmem_call(
        push_kernel,
        (shaped(rows, sensors), shaped(rows, width), shaped(blocks, width, width)),
        in_specs=in_vmem(5),
    )(telemetry, flags, transition, sensing, filter_gain)
    push_in, corr_in, flags_in = vmem_call(
        pair_kernel,
        (shaped(half, width), shaped(blocks, width, width), shaped(segs, 128)),
        [dma((3,)), dma((3,))],
        in_vmem(3), remote=1,
    )(push, corr, wide_flags)
    levels = seg_len.bit_length() - 1
    scalars = pl.BlockSpec(memory_space=pltpu.SMEM)
    powers, ends, local, chunk = vmem_call(
        functools.partial(maps_kernel, seg_len),
        (shaped(levels, half_segs, width, width), shaped(half_segs, width, width),
         shaped(half, width), shaped(width + 8, width)),
        [VMEM((half_segs, width + 8, width), F32)],
        in_vmem(4) + [scalars, scalars] + in_vmem(1),
    )(push, push_in, corr, corr_in, wide_flags, flags_in, transition)
    entry = vmem_call(
        functools.partial(carry_kernel, n),
        shaped(8, width),
        [VMEM((width + 8, width), F32), VMEM((width + 8, width), F32),
         VMEM((GROUP - 1, width + 8, width), F32), VMEM((8, width), F32), VMEM((8, width), F32),
         dma((GROUP + 1,)), dma((GROUP + 1,))],
        in_vmem(2), remote=2,
    )(chunk, start)
    back_levels = half.bit_length() - 1
    drive_scan, gains, shift, final = vmem_call(
        functools.partial(filter_kernel, n, seg_len),
        (shaped(half, width), shaped(back_levels + 1, width, width), shaped(8, width),
         shaped(8, width)),
        [VMEM((half_segs, 8, width), F32), VMEM((half, width), F32)],
        in_vmem(6),
    )(entry, powers, ends, local, transition, smooth_gain)
    smoothed, entry_back = vmem_call(
        functools.partial(smooth_kernel, n),
        (shaped(rows, width), shaped(8, width)),
        [VMEM((2 * n, 8, width), F32), dma((2 * n,)), dma((2 * n + 1,))],
        in_vmem(4), remote=3,
    )(drive_scan, gains, shift, final)
    size = sensors // blocks
    reducers = min(n, REDUCERS)
    high = 2 * width + blocks * (width + size)
    stats, smoothed = vmem_call(
        functools.partial(stats_kernel, n, reducers),
        (shaped(high, width), shaped(rows, width)),
        in_specs=in_vmem(4),
    )(smoothed, entry_back, masked, flags)
    lag, system = vmem_call(
        functools.partial(sum_kernel, n, reducers, blocks),
        (shaped(2 * width, width), shaped(width + size, width)),
        [VMEM((n, high // reducers, width), F32), VMEM((high // reducers, width), F32),
         dma((reducers,)), dma((n,)), dma((n,)), dma((reducers,)),
         dma((n // blocks,)), dma((reducers // blocks,))],
        in_vmem(1), remote=4,
    )(stats)
    new_transition, solved = vmem_call(
        functools.partial(solve_kernel, RIDGE * rows * n),
        (shaped(width, width), shaped(size, width)),
        in_specs=in_vmem(2),
    )(lag, system)
    new_sensing = vmem_call(
        functools.partial(share_kernel, blocks),
        shaped(sensors, width),
        [dma((blocks - 1,)), dma((blocks - 1,))],
        in_vmem(1), remote=5,
    )(solved)
    return (new_transition, new_sensing, smoothed)


def solution(mesh):
    placed = (P("tm", "sens"), P("tm", "sens"), P(), P("sens", None), P(None, "sens"), P(), P())
    return jax.shard_map(
        functools.partial(on_device, mesh.shape["tm"]),
        mesh=mesh,
        in_specs=placed,
        out_specs=(P(), P("sens", None), P("tm", None)),
        check_vma=False,
    )
```

```python
import functools

import jax
import jax.numpy as jnp
from jax import lax
from jax.experimental import pallas as pl
from jax.experimental.pallas import tpu as pltpu
from jax.sharding import PartitionSpec as P

RIDGE = 0.001
GROUP = 4
PIVOT = 32
TOGETHER = 4
REDUCERS = 16
MESH = pl.DeviceIdType.MESH
VMEM = pltpu.VMEM
F32 = jnp.float32
LIMIT = 48 * 1024 * 1024


def terms(x):
    one = x.astype(jnp.bfloat16)
    rest = x - one.astype(F32)
    two = rest.astype(jnp.bfloat16)
    return one, two, (rest - two.astype(F32)).astype(jnp.bfloat16)


def mm(a, b):
    if a.shape[0] % 16 == 0 and a.shape[1] == b.shape[1] == 128:
        a1, a2, a3 = terms(a)
        b1, b2, b3 = terms(b)
        pair = jnp.concatenate([b1, b2], axis=1)
        t = jnp.dot(jnp.concatenate([a1, a2], axis=1), jnp.concatenate([pair, pair], axis=0),
                    preferred_element_type=F32)
        u = jnp.dot(jnp.concatenate([a1, a3], axis=1), jnp.concatenate([b3, b1], axis=0),
                    preferred_element_type=F32)
        return t[:, :128] + (t[:, 128:] + u)
    return jnp.dot(a, b, precision=lax.Precision.HIGHEST, preferred_element_type=F32)


def mv(a, b):
    return jnp.dot(a, b, precision=lax.Precision.HIGH, preferred_element_type=F32)


def mm_tn(a, b):
    return lax.dot_general(
        a, b, (((0,), (0,)), ((), ())),
        precision=lax.Precision.HIGHEST, preferred_element_type=F32,
    )


def mm_nt(a, b):
    return lax.dot_general(
        a, b, (((1,), (1,)), ((), ())),
        precision=lax.Precision.HIGHEST, preferred_element_type=F32,
    )


def row_ids(shape):
    return lax.broadcasted_iota(jnp.int32, shape, 0)


def shift_down(v, by):
    if by % 8 == 0:
        return jnp.concatenate([jnp.zeros((by, v.shape[1]), F32), v[:-by]], axis=0)
    return jnp.where(row_ids(v.shape) >= by, pltpu.roll(v, by, 0), 0.0)


def shift_up(v, by):
    rows = v.shape[0]
    if by % 8 == 0:
        return jnp.concatenate([v[by:], jnp.zeros((by, v.shape[1]), F32)], axis=0)
    return jnp.where(row_ids(v.shape) < rows - by, pltpu.roll(v, rows - by, 0), 0.0)


def vmem_call(body, out_shape, scratch=(), in_specs=None, remote=None):
    params = dict(vmem_limit_bytes=LIMIT)
    if remote is not None:
        params.update(collective_id=remote, has_side_effects=True)
    return pl.pallas_call(
        body,
        out_shape=out_shape,
        in_specs=in_specs,
        out_specs=jax.tree.map(lambda _: pl.BlockSpec(memory_space=VMEM), out_shape),
        scratch_shapes=list(scratch),
        compiler_params=pltpu.CompilerParams(**params),
    )


def in_vmem(count):
    return [pl.BlockSpec(memory_space=VMEM)] * count


def shaped(*shape):
    return jax.ShapeDtypeStruct(shape, F32)


def push_kernel(tele, present, trans, sense, gain, smooth, start,
                masked, push, corr, flags, trans_out, smooth_out, start_out):
    rows, sensors = tele.shape
    blocks, segs = present.shape
    seg_len, width = rows // segs, sensors // blocks
    trans_out[...] = trans[...]
    smooth_out[...] = smooth[...]
    start_out[...] = jnp.broadcast_to(start[...], start_out.shape)

    def placed(columns, each):
        spread = jnp.where(
            lax.broadcasted_iota(jnp.int32, (blocks, columns), 1) // each
            == lax.broadcasted_iota(jnp.int32, (blocks, columns), 0), 1.0, 0.0)
        return lax.dot_general(present[...].astype(F32), spread, (((0,), (0,)), ((), ())),
                               preferred_element_type=F32)

    flags[...] = placed(128, 1)
    wide = placed(sensors, width)
    step = jnp.broadcast_to(wide[:, None, :], (segs, seg_len, sensors)).reshape(rows, sensors)
    values = tele[...] * step
    masked[...] = values
    push[...] = mm_nt(values, gain[...])
    moved = mm(sense[...], trans[...])
    for g in range(blocks):
        part = slice(g * width, (g + 1) * width)
        corr[g] = lax.dot_general(
            moved[part], gain[:, part], (((0,), (1,)), ((), ())),
            precision=lax.Precision.HIGHEST, preferred_element_type=F32)


def remote(src, dst, send, recv, where):
    return pltpu.make_async_remote_copy(
        src_ref=src, dst_ref=dst, send_sem=send, recv_sem=recv,
        device_id=where, device_id_type=MESH)


def pair_kernel(push, corr, flags, push_in, corr_in, flags_in, send, recv):
    tm, core = lax.axis_index("tm"), lax.axis_index("sens")
    other = (tm, 1 - core)
    barrier = pltpu.get_barrier_semaphore()
    pl.semaphore_signal(barrier, inc=1, device_id=other, device_id_type=MESH)
    pl.semaphore_wait(barrier, 1)
    half = push.shape[0] // 2
    theirs = pl.ds(pl.multiple_of((1 - core) * half, half), half)
    copies = [
        remote(corr, corr_in, send.at[0], recv.at[0], other),
        remote(push.at[theirs], push_in, send.at[1], recv.at[1], other),
        remote(flags, flags_in, send.at[2], recv.at[2], other),
    ]
    for copy in copies:
        copy.start()
    for copy in copies:
        copy.wait()


def maps_kernel(seg_len, push, push_in, corr, corr_in, flags, flags_in, trans,
                powers, ends, local, chunk, tree):
    core = lax.axis_index("sens")
    segs = ends.shape[0]
    width = trans.shape[0]
    blocks = corr.shape[0]
    levels = seg_len.bit_length() - 1

    def one(k):
        row = core * segs + k
        q = trans[...].T
        for g in range(blocks):
            q = q - flags[row, g] * corr[g] - flags_in[row, g] * corr_in[g]
        mine = pl.ds(pl.multiple_of(row * seg_len, seg_len), seg_len)
        here = pl.ds(pl.multiple_of(k * seg_len, seg_len), seg_len)
        v = push[mine] + push_in[here]
        for s in range(levels):
            powers[s, k] = q
            t = mm(jnp.concatenate([q, v], axis=0), q)
            v = v + shift_down(t[width:], 1 << s)
            q = t[:width]
        local[here] = v
        ends[k] = q
        tree[k, :width] = q
        tree[k, width:] = jnp.broadcast_to(v[seg_len - 1:], (8, width))

    unroll = 4

    def several(i, carry):
        for j in range(unroll):
            one(i * unroll + j)
        return carry

    lax.fori_loop(0, segs // unroll, several, 0)
    span = 1
    while span < segs:
        for k in range(0, segs, 2 * span):
            tree[k] = compose(tree[k], tree[k + span])
        span *= 2
    chunk[...] = tree[0]


def compose(first, second):
    width = second.shape[1]
    t = mm(first, second[:width])
    return jnp.concatenate([t[:width], t[width:] + second[width:]], axis=0)


def follow(x, step):
    width = step.shape[1]
    return mv(x, step[:width]) + step[width:]


def carry_kernel(n, chunk, start, entry, pair, chip, group, arrived, leaving, send, recv):
    tm, core = lax.axis_index("tm"), lax.axis_index("sens")
    place, mine = lax.rem(tm, GROUP), lax.div(tm, GROUP)
    groups = n // GROUP
    other = (tm, 1 - core)
    base = tm - place
    peers = [(base + lax.rem(place + k, GROUP), core) for k in range(1, GROUP)]
    barrier = pltpu.get_barrier_semaphore()
    chain = [(lax.rem(tm + by, n), core) for by in (GROUP, n - GROUP)]
    for peer in [other] + peers + chain:
        pl.semaphore_signal(barrier, inc=1, device_id=peer, device_id_type=MESH)
    pl.semaphore_wait(barrier, GROUP + 2)

    swap = remote(chunk, pair, send.at[0], recv.at[0], other)
    swap.start()
    swap.wait()
    own, their = chunk[...], pair[...]
    first = jnp.where(core == 0, own, their)
    chip[...] = compose(first, jnp.where(core == 0, their, own))
    copies = []
    for k, peer in enumerate(peers):
        copy = remote(chip, group.at[k], send.at[1 + k], recv.at[1 + k], peer)
        copy.start()
        copies.append(copy)
    for copy in copies:
        copy.wait()
    held = [chip[...]] + [group[k] for k in range(GROUP - 1)]
    ordered = []
    for p in range(GROUP):
        value = held[0]
        for k in range(1, GROUP):
            value = jnp.where(lax.rem(place - k + GROUP, GROUP) == p, held[k], value)
        ordered.append(value)
    low, high = compose(ordered[0], ordered[1]), compose(ordered[2], ordered[3])
    whole = compose(low, high)
    hand = remote(leaving, arrived, send.at[GROUP], recv.at[GROUP], (tm + GROUP, core))

    @pl.when(mine == 0)
    def _():
        arrived[...] = start[...]

    @pl.when(mine > 0)
    def _():
        remote(leaving, arrived, send.at[GROUP], recv.at[GROUP], (tm - GROUP, core)).wait_recv()

    x = arrived[...]
    leaving[...] = follow(x, whole)

    @pl.when(mine < groups - 1)
    def _():
        hand.start()

    x = jnp.where(place >= 2, follow(x, low), x)
    before = jnp.where(place >= 2, ordered[2], ordered[0])
    x = jnp.where(lax.rem(place, 2) == 1, follow(x, before), x)
    entry[...] = jnp.where(core == 1, follow(x, first), x)

    @pl.when(mine < groups - 1)
    def _():
        hand.wait_send()


def filter_kernel(n, seg_len, entry, powers, ends, local, trans, smooth,
                  drive_scan, gains, shift, final, states, filtered):
    levels, segs = powers.shape[:2]
    width = trans.shape[0]
    rows = segs * seg_len

    x = entry[...]
    for k in range(segs):
        states[k] = x
        x = mv(x, ends[k]) + local[(k + 1) * seg_len - 1:(k + 1) * seg_len]

    def one(k):
        here = pl.ds(pl.multiple_of(k * seg_len, seg_len), seg_len)
        w = jnp.concatenate([states[k]] * (seg_len // 8), axis=0)
        ids = row_ids(w.shape)
        for s in range(levels):
            w = jnp.where((ids // (1 << s)) % 2 == 1, mv(w, powers[s, k]), w)
        filtered[here] = local[here] + mv(w, powers[0, k])

    unroll = 4

    def several(i, carry):
        for j in range(unroll):
            one(i * unroll + j)
        return carry

    lax.fori_loop(0, segs // unroll, several, 0)
    f = filtered[...]
    ahead = mm_nt(f, trans[...])
    v = f - mm_nt(ahead, smooth[...])
    last = jnp.broadcast_to(ahead[rows - 1:], (8, width))
    final[...] = last
    p = smooth[...].T
    span, level = 1, 0
    while span < rows:
        gains[level] = p
        t = mm(jnp.concatenate([p, v], axis=0), p)
        v = v + shift_up(t[width:], span)
        p = t[:width]
        span, level = span * 2, level + 1
    gains[level] = p
    drive_scan[...] = v
    is_last = (lax.axis_index("tm") == n - 1) & (lax.axis_index("sens") == 1)
    s = jnp.broadcast_to(v[:1], (8, width))
    shift[...] = jnp.where(is_last, s + mm(last, p), s)


def smooth_kernel(n, drive_scan, gains, shift, final, out, entry, shifts, send, recv):
    tm, core = lax.axis_index("tm"), lax.axis_index("sens")
    chunks = 2 * n
    me = tm * 2 + core
    half, width = drive_scan.shape
    barrier = pltpu.get_barrier_semaphore()

    def place(k):
        c = lax.rem(me + k, chunks)
        return (lax.div(c, 2), lax.rem(c, 2))

    def greet(k, carry):
        pl.semaphore_signal(barrier, inc=1, device_id=place(k), device_id_type=MESH)
        return carry

    lax.fori_loop(1, chunks, greet, 0)
    pl.semaphore_wait(barrier, chunks - 1)

    def launch(k, carry):
        remote(shift, shifts.at[me], send.at[k], recv.at[me], place(k)).start()
        return carry

    lax.fori_loop(1, chunks, launch, 0)
    shifts[me] = shift[...]

    def land(k, carry):
        c = lax.rem(me + k, chunks)
        remote(shift, shifts.at[c], send.at[k], recv.at[c], place(k)).wait()
        return carry

    lax.fori_loop(1, chunks, land, 0)
    v = shifts[:, 0, :]
    levels = gains.shape[0] - 1
    p = gains[levels]
    span = 1
    while span < chunks:
        t = mm(jnp.concatenate([p, v], axis=0), p)
        v = v + shift_up(t[width:], span)
        p = t[:width]
        span *= 2
    x = jnp.sum(jnp.where(row_ids(v.shape) == me + 1, v, 0.0), axis=0, keepdims=True)
    x = jnp.where(me == chunks - 1, final[...], jnp.broadcast_to(x, (8, width)))
    after = jnp.where(row_ids(v.shape) == 2 * tm + 2, v, 0.0)
    entry[...] = jnp.broadcast_to(jnp.sum(after, axis=0, keepdims=True), (8, width))
    w = x
    ids = 7 - row_ids(w.shape)
    for s in range(3):
        w = jnp.where((ids // (1 << s)) % 2 == 1, mv(w, gains[s]), w)
    w = mv(w, gains[0])
    for s in range(3, levels):
        w = jnp.concatenate([mv(w, gains[s]), w], axis=0)
    mine = pl.ds(pl.multiple_of(core * half, half), half)
    out[mine] = drive_scan[...] + w
    swap = remote(out.at[mine], out.at[mine], send.at[0], recv.at[chunks], (tm, 1 - core))
    swap.start()
    swap.wait()


def stats_kernel(n, blocks, reducers, smoothed, entry, masked, flags, stats, smoothed_out):
    rows, width = smoothed.shape
    segs = flags.shape[0]
    seg_len = rows // segs
    sensors = masked.shape[1]
    tm, core = lax.axis_index("tm"), lax.axis_index("sens")
    x = smoothed[...]
    ids = row_ids((rows, width))
    weight = jnp.where((tm == n - 1) & (ids == rows - 1), 0.0, 1.0)
    prior = x * weight
    above = pltpu.roll(x, rows - 1, 0)
    above = jnp.where(ids == rows - 1, jnp.broadcast_to(entry[:1], (rows, width)), above)
    size = sensors // blocks
    cross = mm_tn(masked[...], x)
    smoothed_out[...] = x
    lag = jnp.concatenate([mm_tn(prior, x), mm_tn(above, prior)], axis=0)
    held = []
    for g in range(blocks):
        column = jnp.broadcast_to(flags[:, g:g + 1], (segs, width))
        step = jnp.broadcast_to(column[:, None, :], (segs, seg_len, width)).reshape(rows, width)
        held += [mm_tn(x * step, x), cross[g * size:(g + 1) * size]]
    sensor = jnp.concatenate(held, axis=0)
    lag_piece, piece = lag.shape[0] // reducers, sensor.shape[0] // reducers
    for r in range(reducers):
        at = r * (lag_piece + piece)
        stats[at:at + lag_piece] = lag[r * lag_piece:(r + 1) * lag_piece]
        stats[at + lag_piece:at + lag_piece + piece] = sensor[r * piece:(r + 1) * piece]


def sum_kernel(n, reducers, blocks, stats, lag, system, parts, total,
               send, recv, send2, recv2, send3, recv3):
    me, core = lax.axis_index("tm"), lax.axis_index("sens")
    step = n // reducers
    mine, reduces = me // step, me % step == 0
    lag_piece, piece = lag.shape[0] // reducers, system.shape[0] * blocks // reducers
    per_system = reducers // blocks
    groups = n // blocks
    both = lag_piece + piece
    barrier = pltpu.get_barrier_semaphore()

    def peer(k):
        return lax.rem(me + k, n)

    def greet(k, carry):
        pl.semaphore_signal(barrier, inc=1, device_id=(peer(k), core), device_id_type=MESH)
        return carry

    lax.fori_loop(1, n, greet, 0)
    pl.semaphore_wait(barrier, n - 1)

    def part_of(c):
        return stats.at[pl.ds(pl.multiple_of(c * both, both), both)]

    def give(k):
        c = lax.rem(mine + k, reducers)
        return remote(part_of(c), parts.at[me], send.at[k], recv.at[me], (c * step, core))

    def scatter(k, carry):
        give(k).start()
        return carry

    def sent(k, carry):
        give(k).wait_send()
        return carry

    def land(k, carry):
        c = peer(k)
        remote(part_of(0), parts.at[c], send.at[0], recv.at[c], (c, core)).wait_recv()
        return carry

    lax.fori_loop(1, reducers, scatter, 0)
    if step > 1:
        @pl.when(me % step != 0)
        def _():
            give(0).start()

    task, slot = mine // per_system, mine % per_system
    lag_at = pl.ds(pl.multiple_of(mine * lag_piece, lag_piece), lag_piece)
    system_at = pl.ds(pl.multiple_of(slot * piece, piece), piece)
    lag_part, system_part = total.at[pl.ds(0, lag_piece)], total.at[pl.ds(lag_piece, piece)]

    def tell(k):
        return remote(lag_part, lag.at[lag_at], send2.at[k], recv2.at[mine], (peer(k), core))

    def place(g):
        return lax.rem(me // blocks + g, groups) * blocks + task

    def hand(g):
        return remote(system_part, system.at[system_at], send3.at[g], recv3.at[slot], (place(g), core))

    @pl.when(reduces)
    def _():
        lax.fori_loop(1, n, land, 0)
        parts[me] = part_of(mine)[...]
        total[...] = jnp.sum(parts[...], axis=0)
        lag[lag_at] = total[:lag_piece]

        def spread(g, carry):
            @pl.when(place(g) != me)
            def _():
                hand(g).start()
            return carry

        lax.fori_loop(0, groups, spread, 0)

        @pl.when(me % blocks == task)
        def _():
            system[system_at] = total[lag_piece:]

        def announce(k, carry):
            tell(k).start()
            return carry

        lax.fori_loop(1, n, announce, 0)

    def take(j, carry):
        @pl.when((me % blocks * per_system + j) * step != me)
        def _():
            remote(system_part, system.at[pl.ds(pl.multiple_of(j * piece, piece), piece)],
                   send3.at[0], recv3.at[j], (peer(1), core)).wait_recv()
        return carry

    lax.fori_loop(0, per_system, take, 0)

    def hear(r, carry):
        @pl.when(r * step != me)
        def _():
            remote(lag_part, lag.at[pl.ds(pl.multiple_of(r * lag_piece, lag_piece), lag_piece)],
                   send2.at[0], recv2.at[r], (peer(1), core)).wait_recv()
        return carry

    lax.fori_loop(0, reducers, hear, 0)
    lax.fori_loop(1, reducers, sent, 0)
    if step > 1:
        @pl.when(me % step != 0)
        def _():
            give(0).wait_send()

    @pl.when(reduces)
    def _():
        def told(k, carry):
            tell(k).wait_send()
            return carry

        def handed(g, carry):
            @pl.when(place(g) != me)
            def _():
                hand(g).wait_send()
            return carry

        lax.fori_loop(1, n, told, 0)
        lax.fori_loop(0, groups, handed, 0)


def share_kernel(blocks, solved, new_sensing, send, recv):
    me, core = lax.axis_index("tm"), lax.axis_index("sens")
    size = solved.shape[0]
    task = lax.rem(me, blocks)
    base = me - task
    barrier = pltpu.get_barrier_semaphore()
    peers = [(base + lax.rem(task + k, blocks), core) for k in range(1, blocks)]
    for peer in peers:
        pl.semaphore_signal(barrier, inc=1, device_id=peer, device_id_type=MESH)
    pl.semaphore_wait(barrier, blocks - 1)

    def at(t):
        return pl.ds(pl.multiple_of(t * size, size), size)

    for k, peer in enumerate(peers):
        remote(solved, new_sensing.at[at(task)], send.at[k], recv.at[k], peer).start()
    new_sensing[at(task)] = solved[...]
    for k, peer in enumerate(peers):
        source = lax.rem(task - k - 1 + blocks, blocks)
        remote(solved, new_sensing.at[at(source)], send.at[k], recv.at[k], peer).wait()


def inverse_factor(a):
    count, size = a.shape[:2]
    shape = (count, size, 2 * size)
    wide = (count, 1, 2 * size)
    rows = lax.broadcasted_iota(jnp.int32, shape, 1)
    cols = lax.broadcasted_iota(jnp.int32, shape, 2)
    a = jnp.concatenate([a, jnp.where(rows + size == cols, 1.0, 0.0)[:, :, size:]], axis=2)
    scale = jnp.zeros(shape, F32)
    for k in range(0, size, TOGETHER):
        own = range(TOGETHER)
        pivot = [[jnp.broadcast_to(a[:, k + i:k + i + 1, k + j:k + j + 1], wide) if j >= i else None
                  for j in own] for i in own]
        r = [a[:, k + i:k + i + 1, :] for i in own]
        c = [jnp.broadcast_to(a[:, :, k + i:k + i + 1], shape) for i in own]
        for i in own:
            inv = 1.0 / pivot[i][i]
            scale = jnp.where(rows == k + i, inv, scale)
            for j in range(i + 1, TOGETHER):
                m = pivot[i][j] * inv
                for l in range(j, TOGETHER):
                    pivot[j][l] = pivot[j][l] - m * pivot[i][l]
                r[j] = r[j] - m * r[i]
                c[j] = c[j] - m * c[i]
            a = a - jnp.where(rows > k + i, c[i] * inv, 0.0) * r[i]
    return (a * jnp.sqrt(scale))[:, :, size:]


def solve_kernel(ridge, lag, system, new_transition, solved):
    width = lag.shape[1]
    size = solved.shape[0]
    eye = jnp.where(
        row_ids((width, width)) == lax.broadcasted_iota(jnp.int32, (width, width), 1), ridge, 0.0)
    left = system[width:].T
    left = jnp.concatenate([left] * (width // size), axis=1)
    rest = [jnp.concatenate([lag[:width] + eye, lag[width:].T], axis=1),
            jnp.concatenate([system[:width] + eye, left], axis=1)]
    both = range(2)
    steps = width // PIVOT
    inverses, panels = [], []
    for j in range(steps):
        lo, hi = j * PIVOT, (j + 1) * PIVOT
        inv = inverse_factor(jnp.stack([rest[s][:PIVOT, lo:hi] for s in both]))
        panel = [mm(inv[s], rest[s][:PIVOT]) for s in both]
        inverses.append(inv)
        panels.append(panel)
        if hi < width:
            rest = [rest[s][PIVOT:] - mm_tn(panel[s][:, :width], panel[s])[hi:] for s in both]
    x = [None, None]
    for j in reversed(range(steps)):
        hi = (j + 1) * PIVOT
        for s in both:
            rhs = panels[j][s][:, width:]
            if x[s] is not None:
                full = jnp.concatenate([jnp.zeros((hi, width), F32), x[s]], axis=0)
                rhs = rhs - mm(panels[j][s][:, :width], full)
            piece = mm_tn(inverses[j][s], rhs)
            x[s] = piece if x[s] is None else jnp.concatenate([piece, x[s]], axis=0)
    new_transition[...] = x[0].T
    solved[...] = x[1].T[:size]


def on_device(n, telemetry, present, transition, sensing, filter_gain, smooth_gain, initial_state):
    width = transition.shape[0]
    rows, sensors = telemetry.shape
    segs, blocks = present.shape
    seg_len = rows // segs
    half, half_segs = rows // 2, segs // 2
    dma = pltpu.SemaphoreType.DMA
    masked, push, corr, flags, transition, smooth_gain, start = vmem_call(
        push_kernel,
        (shaped(rows, sensors), shaped(rows, width), shaped(blocks, width, width),
         shaped(segs, 128), shaped(width, width), shaped(width, width), shaped(8, width)),
        in_specs=in_vmem(7),
    )(telemetry, present.T, transition, sensing, filter_gain, smooth_gain, initial_state[None])
    push_in, corr_in, flags_in = vmem_call(
        pair_kernel,
        (shaped(half, width), shaped(blocks, width, width), shaped(segs, 128)),
        [dma((3,)), dma((3,))],
        in_vmem(3), remote=1,
    )(push, corr, flags)
    levels = seg_len.bit_length() - 1
    scalars = pl.BlockSpec(memory_space=pltpu.SMEM)
    powers, ends, local, chunk = vmem_call(
        functools.partial(maps_kernel, seg_len),
        (shaped(levels, half_segs, width, width), shaped(half_segs, width, width),
         shaped(half, width), shaped(width + 8, width)),
        [VMEM((half_segs, width + 8, width), F32)],
        in_vmem(4) + [scalars, scalars] + in_vmem(1),
    )(push, push_in, corr, corr_in, flags, flags_in, transition)
    entry = vmem_call(
        functools.partial(carry_kernel, n),
        shaped(8, width),
        [VMEM((width + 8, width), F32), VMEM((width + 8, width), F32),
         VMEM((GROUP - 1, width + 8, width), F32), VMEM((8, width), F32), VMEM((8, width), F32),
         dma((GROUP + 1,)), dma((GROUP + 1,))],
        in_vmem(2), remote=2,
    )(chunk, start)
    back_levels = half.bit_length() - 1
    drive_scan, gains, shift, final = vmem_call(
        functools.partial(filter_kernel, n, seg_len),
        (shaped(half, width), shaped(back_levels + 1, width, width), shaped(8, width),
         shaped(8, width)),
        [VMEM((half_segs, 8, width), F32), VMEM((half, width), F32)],
        in_vmem(6),
    )(entry, powers, ends, local, transition, smooth_gain)
    smoothed, entry_back = vmem_call(
        functools.partial(smooth_kernel, n),
        (shaped(rows, width), shaped(8, width)),
        [VMEM((2 * n, 8, width), F32), dma((2 * n,)), dma((2 * n + 1,))],
        in_vmem(4), remote=3,
    )(drive_scan, gains, shift, final)
    size = sensors // blocks
    reducers = min(n, REDUCERS)
    high = 2 * width + blocks * (width + size)
    stats, smoothed = vmem_call(
        functools.partial(stats_kernel, n, blocks, reducers),
        (shaped(high, width), shaped(rows, width)),
        in_specs=in_vmem(4),
    )(smoothed, entry_back, masked, flags)
    lag, system = vmem_call(
        functools.partial(sum_kernel, n, reducers, blocks),
        (shaped(2 * width, width), shaped(width + size, width)),
        [VMEM((n, high // reducers, width), F32), VMEM((high // reducers, width), F32),
         dma((reducers,)), dma((n,)), dma((n,)), dma((reducers,)),
         dma((n // blocks,)), dma((reducers // blocks,))],
        in_vmem(1), remote=4,
    )(stats)
    new_transition, solved = vmem_call(
        functools.partial(solve_kernel, RIDGE * rows * n),
        (shaped(width, width), shaped(size, width)),
        in_specs=in_vmem(2),
    )(lag, system)
    new_sensing = vmem_call(
        functools.partial(share_kernel, blocks),
        shaped(sensors, width),
        [dma((blocks - 1,)), dma((blocks - 1,))],
        in_vmem(1), remote=5,
    )(solved)
    return (new_transition, new_sensing, smoothed)


def solution(mesh):
    placed = (P("tm", "sens"), P("tm", "sens"), P(), P("sens", None), P(None, "sens"), P(), P())
    return jax.shard_map(
        functools.partial(on_device, mesh.shape["tm"]),
        mesh=mesh,
        in_specs=placed,
        out_specs=(P(), P("sens", None), P("tm", None)),
        check_vma=False,
    )
```

```python
import functools

import jax
import jax.numpy as jnp
from jax import lax
from jax.experimental import pallas as pl
from jax.experimental.pallas import tpu as pltpu
from jax.sharding import PartitionSpec as P

RIDGE = 0.001
GROUP = 4
PIVOT = 32
TOGETHER = 4
REDUCERS = 16
MESH = pl.DeviceIdType.MESH
VMEM = pltpu.VMEM
F32 = jnp.float32
LIMIT = 48 * 1024 * 1024


def terms(x):
    one = x.astype(jnp.bfloat16)
    rest = x - one.astype(F32)
    two = rest.astype(jnp.bfloat16)
    return one, two, (rest - two.astype(F32)).astype(jnp.bfloat16)


def mm(a, b):
    if a.shape[0] % 16 == 0 and a.shape[1] == b.shape[1] == 128:
        a1, a2, a3 = terms(a)
        b1, b2, b3 = terms(b)
        pair = jnp.concatenate([b1, b2], axis=1)
        t = jnp.dot(jnp.concatenate([a1, a2], axis=1), jnp.concatenate([pair, pair], axis=0),
                    preferred_element_type=F32)
        u = jnp.dot(jnp.concatenate([a1, a3], axis=1), jnp.concatenate([b3, b1], axis=0),
                    preferred_element_type=F32)
        return t[:, :128] + (t[:, 128:] + u)
    return jnp.dot(a, b, precision=lax.Precision.HIGHEST, preferred_element_type=F32)


def mv(a, b):
    return jnp.dot(a, b, precision=lax.Precision.HIGH, preferred_element_type=F32)


def mm_tn(a, b):
    return lax.dot_general(
        a, b, (((0,), (0,)), ((), ())),
        precision=lax.Precision.HIGHEST, preferred_element_type=F32,
    )


def mm_nt(a, b):
    return lax.dot_general(
        a, b, (((1,), (1,)), ((), ())),
        precision=lax.Precision.HIGHEST, preferred_element_type=F32,
    )


def row_ids(shape):
    return lax.broadcasted_iota(jnp.int32, shape, 0)


def shift_down(v, by):
    if by % 8 == 0:
        return jnp.concatenate([jnp.zeros((by, v.shape[1]), F32), v[:-by]], axis=0)
    return jnp.where(row_ids(v.shape) >= by, pltpu.roll(v, by, 0), 0.0)


def shift_up(v, by):
    rows = v.shape[0]
    if by % 8 == 0:
        return jnp.concatenate([v[by:], jnp.zeros((by, v.shape[1]), F32)], axis=0)
    return jnp.where(row_ids(v.shape) < rows - by, pltpu.roll(v, rows - by, 0), 0.0)


def vmem_call(body, out_shape, scratch=(), in_specs=None, remote=None):
    params = dict(vmem_limit_bytes=LIMIT)
    if remote is not None:
        params.update(collective_id=remote, has_side_effects=True)
    return pl.pallas_call(
        body,
        out_shape=out_shape,
        in_specs=in_specs,
        out_specs=jax.tree.map(lambda _: pl.BlockSpec(memory_space=VMEM), out_shape),
        scratch_shapes=list(scratch),
        compiler_params=pltpu.CompilerParams(**params),
    )


def in_vmem(count):
    return [pl.BlockSpec(memory_space=VMEM)] * count


def shaped(*shape):
    return jax.ShapeDtypeStruct(shape, F32)


def push_kernel(tele, present, trans, sense, gain, smooth, start,
                masked, push, corr, flags, trans_out, smooth_out, start_out):
    rows, sensors = tele.shape
    blocks, segs = present.shape
    seg_len, width = rows // segs, sensors // blocks
    trans_out[...] = trans[...]
    smooth_out[...] = smooth[...]
    start_out[...] = jnp.broadcast_to(start[...], start_out.shape)

    def placed(columns, each):
        spread = jnp.where(
            lax.broadcasted_iota(jnp.int32, (blocks, columns), 1) // each
            == lax.broadcasted_iota(jnp.int32, (blocks, columns), 0), 1.0, 0.0)
        return lax.dot_general(present[...].astype(F32), spread, (((0,), (0,)), ((), ())),
                               preferred_element_type=F32)

    flags[...] = placed(128, 1)
    wide = placed(sensors, width)
    step = jnp.broadcast_to(wide[:, None, :], (segs, seg_len, sensors)).reshape(rows, sensors)
    values = tele[...] * step
    masked[...] = values
    push[...] = mm_nt(values, gain[...])
    moved = mm(sense[...], trans[...])
    for g in range(blocks):
        part = slice(g * width, (g + 1) * width)
        corr[g] = lax.dot_general(
            moved[part], gain[:, part], (((0,), (1,)), ((), ())),
            precision=lax.Precision.HIGHEST, preferred_element_type=F32)


def remote(src, dst, send, recv, where):
    return pltpu.make_async_remote_copy(
        src_ref=src, dst_ref=dst, send_sem=send, recv_sem=recv,
        device_id=where, device_id_type=MESH)


def pair_kernel(push, corr, flags, push_in, corr_in, flags_in, send, recv):
    tm, core = lax.axis_index("tm"), lax.axis_index("sens")
    other = (tm, 1 - core)
    barrier = pltpu.get_barrier_semaphore()
    pl.semaphore_signal(barrier, inc=1, device_id=other, device_id_type=MESH)
    pl.semaphore_wait(barrier, 1)
    half = push.shape[0] // 2
    theirs = pl.ds(pl.multiple_of((1 - core) * half, half), half)
    copies = [
        remote(corr, corr_in, send.at[0], recv.at[0], other),
        remote(push.at[theirs], push_in, send.at[1], recv.at[1], other),
        remote(flags, flags_in, send.at[2], recv.at[2], other),
    ]
    for copy in copies:
        copy.start()
    for copy in copies:
        copy.wait()


def maps_kernel(seg_len, push, push_in, corr, corr_in, flags, flags_in, trans,
                powers, ends, local, chunk, tree):
    core = lax.axis_index("sens")
    segs = ends.shape[0]
    width = trans.shape[0]
    blocks = corr.shape[0]
    levels = seg_len.bit_length() - 1

    together = 4

    def several(i, carry):
        ks = [i * together + j for j in range(together)]
        here = [pl.ds(pl.multiple_of(k * seg_len, seg_len), seg_len) for k in ks]
        qs, vs = [], []
        for k, at in zip(ks, here):
            row = core * segs + k
            q = trans[...].T
            for g in range(blocks):
                q = q - flags[row, g] * corr[g] - flags_in[row, g] * corr_in[g]
            mine = pl.ds(pl.multiple_of(row * seg_len, seg_len), seg_len)
            qs.append(q)
            vs.append(push[mine] + push_in[at])
        for s in range(levels):
            ts = [mm(jnp.concatenate([q, v], axis=0), q) for q, v in zip(qs, vs)]
            for k, q in zip(ks, qs):
                powers[s, k] = q
            vs = [v + shift_down(t[width:], 1 << s) for t, v in zip(ts, vs)]
            qs = [t[:width] for t in ts]
        for k, at, q, v in zip(ks, here, qs, vs):
            local[at] = v
            ends[k] = q
            tree[k, :width] = q
            tree[k, width:] = jnp.broadcast_to(v[seg_len - 1:], (8, width))
        return carry

    lax.fori_loop(0, segs // together, several, 0)
    span = 1
    while span < segs:
        for k in range(0, segs, 2 * span):
            tree[k] = compose(tree[k], tree[k + span])
        span *= 2
    chunk[...] = tree[0]


def compose(first, second):
    width = second.shape[1]
    t = mm(first, second[:width])
    return jnp.concatenate([t[:width], t[width:] + second[width:]], axis=0)


def follow(x, step):
    width = step.shape[1]
    return mv(x, step[:width]) + step[width:]


def carry_kernel(n, chunk, start, entry, pair, chip, group, arrived, leaving, send, recv):
    tm, core = lax.axis_index("tm"), lax.axis_index("sens")
    place, mine = lax.rem(tm, GROUP), lax.div(tm, GROUP)
    groups = n // GROUP
    other = (tm, 1 - core)
    base = tm - place
    peers = [(base + lax.rem(place + k, GROUP), core) for k in range(1, GROUP)]
    barrier = pltpu.get_barrier_semaphore()
    chain = [(lax.rem(tm + by, n), core) for by in (GROUP, n - GROUP)]
    for peer in [other] + peers + chain:
        pl.semaphore_signal(barrier, inc=1, device_id=peer, device_id_type=MESH)
    pl.semaphore_wait(barrier, GROUP + 2)

    swap = remote(chunk, pair, send.at[0], recv.at[0], other)
    swap.start()
    swap.wait()
    own, their = chunk[...], pair[...]
    first = jnp.where(core == 0, own, their)
    chip[...] = compose(first, jnp.where(core == 0, their, own))
    copies = []
    for k, peer in enumerate(peers):
        copy = remote(chip, group.at[k], send.at[1 + k], recv.at[1 + k], peer)
        copy.start()
        copies.append(copy)
    for copy in copies:
        copy.wait()
    held = [chip[...]] + [group[k] for k in range(GROUP - 1)]
    ordered = []
    for p in range(GROUP):
        value = held[0]
        for k in range(1, GROUP):
            value = jnp.where(lax.rem(place - k + GROUP, GROUP) == p, held[k], value)
        ordered.append(value)
    low, high = compose(ordered[0], ordered[1]), compose(ordered[2], ordered[3])
    whole = compose(low, high)
    hand = remote(leaving, arrived, send.at[GROUP], recv.at[GROUP], (tm + GROUP, core))

    @pl.when(mine == 0)
    def _():
        arrived[...] = start[...]

    @pl.when(mine > 0)
    def _():
        remote(leaving, arrived, send.at[GROUP], recv.at[GROUP], (tm - GROUP, core)).wait_recv()

    x = arrived[...]
    leaving[...] = follow(x, whole)

    @pl.when(mine < groups - 1)
    def _():
        hand.start()

    x = jnp.where(place >= 2, follow(x, low), x)
    before = jnp.where(place >= 2, ordered[2], ordered[0])
    x = jnp.where(lax.rem(place, 2) == 1, follow(x, before), x)
    entry[...] = jnp.where(core == 1, follow(x, first), x)

    @pl.when(mine < groups - 1)
    def _():
        hand.wait_send()


def filter_kernel(n, seg_len, entry, powers, ends, local, trans, smooth,
                  drive_scan, gains, shift, final, states, filtered):
    levels, segs = powers.shape[:2]
    width = trans.shape[0]
    rows = segs * seg_len

    x = entry[...]
    for k in range(segs):
        states[k] = x
        x = mv(x, ends[k]) + local[(k + 1) * seg_len - 1:(k + 1) * seg_len]

    together = 8

    def several(i, carry):
        ks = [i * together + j for j in range(together)]
        ws = [jnp.concatenate([states[k]] * (seg_len // 8), axis=0) for k in ks]
        ids = row_ids(ws[0].shape)
        for s in range(levels):
            ws = [jnp.where((ids // (1 << s)) % 2 == 1, mv(w, powers[s, k]), w)
                  for k, w in zip(ks, ws)]
        ws = [mv(w, powers[0, k]) for k, w in zip(ks, ws)]
        for k, w in zip(ks, ws):
            here = pl.ds(pl.multiple_of(k * seg_len, seg_len), seg_len)
            filtered[here] = local[here] + w
        return carry

    lax.fori_loop(0, segs // together, several, 0)
    f = filtered[...]
    ahead = mm_nt(f, trans[...])
    v = f - mm_nt(ahead, smooth[...])
    last = jnp.broadcast_to(ahead[rows - 1:], (8, width))
    final[...] = last
    p = smooth[...].T
    span, level = 1, 0
    while span < rows:
        gains[level] = p
        t = mm(jnp.concatenate([p, v], axis=0), p)
        v = v + shift_up(t[width:], span)
        p = t[:width]
        span, level = span * 2, level + 1
    gains[level] = p
    drive_scan[...] = v
    is_last = (lax.axis_index("tm") == n - 1) & (lax.axis_index("sens") == 1)
    s = jnp.broadcast_to(v[:1], (8, width))
    shift[...] = jnp.where(is_last, s + mm(last, p), s)


def smooth_kernel(n, drive_scan, gains, shift, final, out, entry, shifts, send, recv):
    tm, core = lax.axis_index("tm"), lax.axis_index("sens")
    chunks = 2 * n
    me = tm * 2 + core
    half, width = drive_scan.shape
    barrier = pltpu.get_barrier_semaphore()

    def place(k):
        c = lax.rem(me + k, chunks)
        return (lax.div(c, 2), lax.rem(c, 2))

    def greet(k, carry):
        pl.semaphore_signal(barrier, inc=1, device_id=place(k), device_id_type=MESH)
        return carry

    lax.fori_loop(1, chunks, greet, 0)
    pl.semaphore_wait(barrier, chunks - 1)

    def launch(k, carry):
        remote(shift, shifts.at[me], send.at[k], recv.at[me], place(k)).start()
        return carry

    lax.fori_loop(1, chunks, launch, 0)
    shifts[me] = shift[...]

    def land(k, carry):
        c = lax.rem(me + k, chunks)
        remote(shift, shifts.at[c], send.at[k], recv.at[c], place(k)).wait()
        return carry

    lax.fori_loop(1, chunks, land, 0)
    v = shifts[:, 0, :]
    levels = gains.shape[0] - 1
    p = gains[levels]
    span = 1
    while span < chunks:
        t = mm(jnp.concatenate([p, v], axis=0), p)
        v = v + shift_up(t[width:], span)
        p = t[:width]
        span *= 2
    x = jnp.sum(jnp.where(row_ids(v.shape) == me + 1, v, 0.0), axis=0, keepdims=True)
    x = jnp.where(me == chunks - 1, final[...], jnp.broadcast_to(x, (8, width)))
    after = jnp.where(row_ids(v.shape) == 2 * tm + 2, v, 0.0)
    entry[...] = jnp.broadcast_to(jnp.sum(after, axis=0, keepdims=True), (8, width))
    w = x
    ids = 7 - row_ids(w.shape)
    for s in range(3):
        w = jnp.where((ids // (1 << s)) % 2 == 1, mv(w, gains[s]), w)
    w = mv(w, gains[0])
    for s in range(3, levels):
        w = jnp.concatenate([mv(w, gains[s]), w], axis=0)
    mine = pl.ds(pl.multiple_of(core * half, half), half)
    out[mine] = drive_scan[...] + w
    swap = remote(out.at[mine], out.at[mine], send.at[0], recv.at[chunks], (tm, 1 - core))
    swap.start()
    swap.wait()


def stats_kernel(n, blocks, reducers, smoothed, entry, masked, flags, stats, smoothed_out):
    rows, width = smoothed.shape
    segs = flags.shape[0]
    seg_len = rows // segs
    sensors = masked.shape[1]
    tm, core = lax.axis_index("tm"), lax.axis_index("sens")
    x = smoothed[...]
    ids = row_ids((rows, width))
    weight = jnp.where((tm == n - 1) & (ids == rows - 1), 0.0, 1.0)
    prior = x * weight
    above = pltpu.roll(x, rows - 1, 0)
    above = jnp.where(ids == rows - 1, jnp.broadcast_to(entry[:1], (rows, width)), above)
    size = sensors // blocks
    cross = mm_tn(masked[...], x)
    smoothed_out[...] = x
    lag = jnp.concatenate([mm_tn(prior, x), mm_tn(above, prior)], axis=0)
    held = []
    for g in range(blocks):
        column = jnp.broadcast_to(flags[:, g:g + 1], (segs, width))
        step = jnp.broadcast_to(column[:, None, :], (segs, seg_len, width)).reshape(rows, width)
        held += [mm_tn(x * step, x), cross[g * size:(g + 1) * size]]
    sensor = jnp.concatenate(held, axis=0)
    lag_piece, piece = lag.shape[0] // reducers, sensor.shape[0] // reducers
    for r in range(reducers):
        at = r * (lag_piece + piece)
        stats[at:at + lag_piece] = lag[r * lag_piece:(r + 1) * lag_piece]
        stats[at + lag_piece:at + lag_piece + piece] = sensor[r * piece:(r + 1) * piece]


def sum_kernel(n, reducers, blocks, stats, lag, system, parts, total,
               send, recv, send2, recv2, send3, recv3):
    me, core = lax.axis_index("tm"), lax.axis_index("sens")
    step = n // reducers
    mine, reduces = me // step, me % step == 0
    lag_piece, piece = lag.shape[0] // reducers, system.shape[0] * blocks // reducers
    per_system = reducers // blocks
    groups = n // blocks
    both = lag_piece + piece
    barrier = pltpu.get_barrier_semaphore()

    def peer(k):
        return lax.rem(me + k, n)

    def greet(k, carry):
        pl.semaphore_signal(barrier, inc=1, device_id=(peer(k), core), device_id_type=MESH)
        return carry

    lax.fori_loop(1, n, greet, 0)
    pl.semaphore_wait(barrier, n - 1)

    def part_of(c):
        return stats.at[pl.ds(pl.multiple_of(c * both, both), both)]

    def give(k):
        c = lax.rem(mine + k, reducers)
        return remote(part_of(c), parts.at[me], send.at[k], recv.at[me], (c * step, core))

    def scatter(k, carry):
        give(k).start()
        return carry

    def sent(k, carry):
        give(k).wait_send()
        return carry

    def land(k, carry):
        c = peer(k)
        remote(part_of(0), parts.at[c], send.at[0], recv.at[c], (c, core)).wait_recv()
        return carry

    lax.fori_loop(1, reducers, scatter, 0)
    if step > 1:
        @pl.when(me % step != 0)
        def _():
            give(0).start()

    task, slot = mine // per_system, mine % per_system
    lag_at = pl.ds(pl.multiple_of(mine * lag_piece, lag_piece), lag_piece)
    system_at = pl.ds(pl.multiple_of(slot * piece, piece), piece)
    lag_part, system_part = total.at[pl.ds(0, lag_piece)], total.at[pl.ds(lag_piece, piece)]

    def tell(k):
        return remote(lag_part, lag.at[lag_at], send2.at[k], recv2.at[mine], (peer(k), core))

    def place(g):
        return lax.rem(me // blocks + g, groups) * blocks + task

    def hand(g):
        return remote(system_part, system.at[system_at], send3.at[g], recv3.at[slot], (place(g), core))

    @pl.when(reduces)
    def _():
        lax.fori_loop(1, n, land, 0)
        parts[me] = part_of(mine)[...]
        total[...] = jnp.sum(parts[...], axis=0)
        lag[lag_at] = total[:lag_piece]

        def spread(g, carry):
            @pl.when(place(g) != me)
            def _():
                hand(g).start()
            return carry

        lax.fori_loop(0, groups, spread, 0)

        @pl.when(me % blocks == task)
        def _():
            system[system_at] = total[lag_piece:]

        def announce(k, carry):
            tell(k).start()
            return carry

        lax.fori_loop(1, n, announce, 0)

    def take(j, carry):
        @pl.when((me % blocks * per_system + j) * step != me)
        def _():
            remote(system_part, system.at[pl.ds(pl.multiple_of(j * piece, piece), piece)],
                   send3.at[0], recv3.at[j], (peer(1), core)).wait_recv()
        return carry

    lax.fori_loop(0, per_system, take, 0)

    def hear(r, carry):
        @pl.when(r * step != me)
        def _():
            remote(lag_part, lag.at[pl.ds(pl.multiple_of(r * lag_piece, lag_piece), lag_piece)],
                   send2.at[0], recv2.at[r], (peer(1), core)).wait_recv()
        return carry

    lax.fori_loop(0, reducers, hear, 0)
    lax.fori_loop(1, reducers, sent, 0)
    if step > 1:
        @pl.when(me % step != 0)
        def _():
            give(0).wait_send()

    @pl.when(reduces)
    def _():
        def told(k, carry):
            tell(k).wait_send()
            return carry

        def handed(g, carry):
            @pl.when(place(g) != me)
            def _():
                hand(g).wait_send()
            return carry

        lax.fori_loop(1, n, told, 0)
        lax.fori_loop(0, groups, handed, 0)


def share_kernel(blocks, solved, new_sensing, send, recv):
    me, core = lax.axis_index("tm"), lax.axis_index("sens")
    size = solved.shape[0]
    task = lax.rem(me, blocks)
    base = me - task
    barrier = pltpu.get_barrier_semaphore()
    peers = [(base + lax.rem(task + k, blocks), core) for k in range(1, blocks)]
    for peer in peers:
        pl.semaphore_signal(barrier, inc=1, device_id=peer, device_id_type=MESH)
    pl.semaphore_wait(barrier, blocks - 1)

    def at(t):
        return pl.ds(pl.multiple_of(t * size, size), size)

    for k, peer in enumerate(peers):
        remote(solved, new_sensing.at[at(task)], send.at[k], recv.at[k], peer).start()
    new_sensing[at(task)] = solved[...]
    for k, peer in enumerate(peers):
        source = lax.rem(task - k - 1 + blocks, blocks)
        remote(solved, new_sensing.at[at(source)], send.at[k], recv.at[k], peer).wait()


def inverse_factor(a):
    count, size = a.shape[:2]
    shape = (count, size, 2 * size)
    wide = (count, 1, 2 * size)
    rows = lax.broadcasted_iota(jnp.int32, shape, 1)
    cols = lax.broadcasted_iota(jnp.int32, shape, 2)
    a = jnp.concatenate([a, jnp.where(rows + size == cols, 1.0, 0.0)[:, :, size:]], axis=2)
    scale = jnp.zeros(shape, F32)
    for k in range(0, size, TOGETHER):
        own = range(TOGETHER)
        pivot = [[jnp.broadcast_to(a[:, k + i:k + i + 1, k + j:k + j + 1], wide) if j >= i else None
                  for j in own] for i in own]
        r = [a[:, k + i:k + i + 1, :] for i in own]
        c = [jnp.broadcast_to(a[:, :, k + i:k + i + 1], shape) for i in own]
        for i in own:
            inv = 1.0 / pivot[i][i]
            scale = jnp.where(rows == k + i, inv, scale)
            for j in range(i + 1, TOGETHER):
                m = pivot[i][j] * inv
                for l in range(j, TOGETHER):
                    pivot[j][l] = pivot[j][l] - m * pivot[i][l]
                r[j] = r[j] - m * r[i]
                c[j] = c[j] - m * c[i]
            a = a - jnp.where(rows > k + i, c[i] * inv, 0.0) * r[i]
    return (a * jnp.sqrt(scale))[:, :, size:]


def solve_kernel(ridge, lag, system, new_transition, solved):
    width = lag.shape[1]
    size = solved.shape[0]
    eye = jnp.where(
        row_ids((width, width)) == lax.broadcasted_iota(jnp.int32, (width, width), 1), ridge, 0.0)
    left = system[width:].T
    left = jnp.concatenate([left] * (width // size), axis=1)
    rest = [jnp.concatenate([lag[:width] + eye, lag[width:].T], axis=1),
            jnp.concatenate([system[:width] + eye, left], axis=1)]
    both = range(2)
    steps = width // PIVOT
    inverses, panels = [], []
    for j in range(steps):
        lo, hi = j * PIVOT, (j + 1) * PIVOT
        inv = inverse_factor(jnp.stack([rest[s][:PIVOT, lo:hi] for s in both]))
        panel = [mm(inv[s], rest[s][:PIVOT]) for s in both]
        inverses.append(inv)
        panels.append(panel)
        if hi < width:
            rest = [rest[s][PIVOT:] - mm_tn(panel[s][:, :width], panel[s])[hi:] for s in both]
    x = [None, None]
    for j in reversed(range(steps)):
        hi = (j + 1) * PIVOT
        for s in both:
            rhs = panels[j][s][:, width:]
            if x[s] is not None:
                full = jnp.concatenate([jnp.zeros((hi, width), F32), x[s]], axis=0)
                rhs = rhs - mm(panels[j][s][:, :width], full)
            piece = mm_tn(inverses[j][s], rhs)
            x[s] = piece if x[s] is None else jnp.concatenate([piece, x[s]], axis=0)
    new_transition[...] = x[0].T
    solved[...] = x[1].T[:size]


def on_device(n, telemetry, present, transition, sensing, filter_gain, smooth_gain, initial_state):
    width = transition.shape[0]
    rows, sensors = telemetry.shape
    segs, blocks = present.shape
    seg_len = rows // segs
    half, half_segs = rows // 2, segs // 2
    dma = pltpu.SemaphoreType.DMA
    masked, push, corr, flags, transition, smooth_gain, start = vmem_call(
        push_kernel,
        (shaped(rows, sensors), shaped(rows, width), shaped(blocks, width, width),
         shaped(segs, 128), shaped(width, width), shaped(width, width), shaped(8, width)),
        in_specs=in_vmem(7),
    )(telemetry, present.T, transition, sensing, filter_gain, smooth_gain, initial_state[None])
    push_in, corr_in, flags_in = vmem_call(
        pair_kernel,
        (shaped(half, width), shaped(blocks, width, width), shaped(segs, 128)),
        [dma((3,)), dma((3,))],
        in_vmem(3), remote=1,
    )(push, corr, flags)
    levels = seg_len.bit_length() - 1
    scalars = pl.BlockSpec(memory_space=pltpu.SMEM)
    powers, ends, local, chunk = vmem_call(
        functools.partial(maps_kernel, seg_len),
        (shaped(levels, half_segs, width, width), shaped(half_segs, width, width),
         shaped(half, width), shaped(width + 8, width)),
        [VMEM((half_segs, width + 8, width), F32)],
        in_vmem(4) + [scalars, scalars] + in_vmem(1),
    )(push, push_in, corr, corr_in, flags, flags_in, transition)
    entry = vmem_call(
        functools.partial(carry_kernel, n),
        shaped(8, width),
        [VMEM((width + 8, width), F32), VMEM((width + 8, width), F32),
         VMEM((GROUP - 1, width + 8, width), F32), VMEM((8, width), F32), VMEM((8, width), F32),
         dma((GROUP + 1,)), dma((GROUP + 1,))],
        in_vmem(2), remote=2,
    )(chunk, start)
    back_levels = half.bit_length() - 1
    drive_scan, gains, shift, final = vmem_call(
        functools.partial(filter_kernel, n, seg_len),
        (shaped(half, width), shaped(back_levels + 1, width, width), shaped(8, width),
         shaped(8, width)),
        [VMEM((half_segs, 8, width), F32), VMEM((half, width), F32)],
        in_vmem(6),
    )(entry, powers, ends, local, transition, smooth_gain)
    smoothed, entry_back = vmem_call(
        functools.partial(smooth_kernel, n),
        (shaped(rows, width), shaped(8, width)),
        [VMEM((2 * n, 8, width), F32), dma((2 * n,)), dma((2 * n + 1,))],
        in_vmem(4), remote=3,
    )(drive_scan, gains, shift, final)
    size = sensors // blocks
    reducers = min(n, REDUCERS)
    high = 2 * width + blocks * (width + size)
    stats, smoothed = vmem_call(
        functools.partial(stats_kernel, n, blocks, reducers),
        (shaped(high, width), shaped(rows, width)),
        in_specs=in_vmem(4),
    )(smoothed, entry_back, masked, flags)
    lag, system = vmem_call(
        functools.partial(sum_kernel, n, reducers, blocks),
        (shaped(2 * width, width), shaped(width + size, width)),
        [VMEM((n, high // reducers, width), F32), VMEM((high // reducers, width), F32),
         dma((reducers,)), dma((n,)), dma((n,)), dma((reducers,)),
         dma((n // blocks,)), dma((reducers // blocks,))],
        in_vmem(1), remote=4,
    )(stats)
    new_transition, solved = vmem_call(
        functools.partial(solve_kernel, RIDGE * rows * n),
        (shaped(width, width), shaped(size, width)),
        in_specs=in_vmem(2),
    )(lag, system)
    new_sensing = vmem_call(
        functools.partial(share_kernel, blocks),
        shaped(sensors, width),
        [dma((blocks - 1,)), dma((blocks - 1,))],
        in_vmem(1), remote=5,
    )(solved)
    return (new_transition, new_sensing, smoothed)


def solution(mesh):
    placed = (P("tm", "sens"), P("tm", "sens"), P(), P("sens", None), P(None, "sens"), P(), P())
    return jax.shard_map(
        functools.partial(on_device, mesh.shape["tm"]),
        mesh=mesh,
        in_specs=placed,
        out_specs=(P(), P("sens", None), P("tm", None)),
        check_vma=False,
    )
```

```python
import functools

import jax
import jax.numpy as jnp
from jax import lax
from jax.experimental import pallas as pl
from jax.experimental.pallas import tpu as pltpu
from jax.sharding import PartitionSpec as P

RIDGE = 0.001
GROUP = 4
PIVOT = 32
TOGETHER = 4
REDUCERS = 16
MESH = pl.DeviceIdType.MESH
VMEM = pltpu.VMEM
F32 = jnp.float32
LIMIT = 48 * 1024 * 1024


def terms(x):
    one = x.astype(jnp.bfloat16)
    rest = x - one.astype(F32)
    two = rest.astype(jnp.bfloat16)
    return one, two, (rest - two.astype(F32)).astype(jnp.bfloat16)


def mm(a, b):
    if a.shape[0] % 16 == 0 and a.shape[1] == b.shape[1] == 128:
        a1, a2, a3 = terms(a)
        b1, b2, b3 = terms(b)
        pair = jnp.concatenate([b1, b2], axis=1)
        t = jnp.dot(jnp.concatenate([a1, a2], axis=1), jnp.concatenate([pair, pair], axis=0),
                    preferred_element_type=F32)
        u = jnp.dot(jnp.concatenate([a1, a3], axis=1), jnp.concatenate([b3, b1], axis=0),
                    preferred_element_type=F32)
        return t[:, :128] + (t[:, 128:] + u)
    return jnp.dot(a, b, precision=lax.Precision.HIGHEST, preferred_element_type=F32)


def mv(a, b):
    return jnp.dot(a, b, precision=lax.Precision.HIGH, preferred_element_type=F32)


def mm_tn(a, b):
    return lax.dot_general(
        a, b, (((0,), (0,)), ((), ())),
        precision=lax.Precision.HIGHEST, preferred_element_type=F32,
    )


def mm_nt(a, b):
    return lax.dot_general(
        a, b, (((1,), (1,)), ((), ())),
        precision=lax.Precision.HIGHEST, preferred_element_type=F32,
    )


def row_ids(shape):
    return lax.broadcasted_iota(jnp.int32, shape, 0)


def shift_down(v, by):
    if by % 8 == 0:
        return jnp.concatenate([jnp.zeros((by, v.shape[1]), F32), v[:-by]], axis=0)
    return jnp.where(row_ids(v.shape) >= by, pltpu.roll(v, by, 0), 0.0)


def shift_up(v, by):
    rows = v.shape[0]
    if by % 8 == 0:
        return jnp.concatenate([v[by:], jnp.zeros((by, v.shape[1]), F32)], axis=0)
    return jnp.where(row_ids(v.shape) < rows - by, pltpu.roll(v, rows - by, 0), 0.0)


def vmem_call(body, out_shape, scratch=(), in_specs=None, remote=None):
    params = dict(vmem_limit_bytes=LIMIT)
    if remote is not None:
        params.update(collective_id=remote, has_side_effects=True)
    return pl.pallas_call(
        body,
        out_shape=out_shape,
        in_specs=in_specs,
        out_specs=jax.tree.map(lambda _: pl.BlockSpec(memory_space=VMEM), out_shape),
        scratch_shapes=list(scratch),
        compiler_params=pltpu.CompilerParams(**params),
    )


def in_vmem(count):
    return [pl.BlockSpec(memory_space=VMEM)] * count


def shaped(*shape):
    return jax.ShapeDtypeStruct(shape, F32)


def push_kernel(tele, present, trans, sense, gain, smooth, start,
                masked, push, corr, flags, trans_out, smooth_out, start_out):
    rows, sensors = tele.shape
    blocks, segs = present.shape
    seg_len, width = rows // segs, sensors // blocks
    trans_out[...] = trans[...]
    smooth_out[...] = smooth[...]
    start_out[...] = jnp.broadcast_to(start[...], start_out.shape)

    def placed(columns, each):
        spread = jnp.where(
            lax.broadcasted_iota(jnp.int32, (blocks, columns), 1) // each
            == lax.broadcasted_iota(jnp.int32, (blocks, columns), 0), 1.0, 0.0)
        return lax.dot_general(present[...].astype(F32), spread, (((0,), (0,)), ((), ())),
                               preferred_element_type=F32)

    flags[...] = placed(128, 1)
    wide = placed(sensors, width)
    step = jnp.broadcast_to(wide[:, None, :], (segs, seg_len, sensors)).reshape(rows, sensors)
    values = tele[...] * step
    masked[...] = values
    push[...] = mm_nt(values, gain[...])
    moved = mm(sense[...], trans[...])
    for g in range(blocks):
        part = slice(g * width, (g + 1) * width)
        corr[g] = lax.dot_general(
            moved[part], gain[:, part], (((0,), (1,)), ((), ())),
            precision=lax.Precision.HIGHEST, preferred_element_type=F32)


def remote(src, dst, send, recv, where):
    return pltpu.make_async_remote_copy(
        src_ref=src, dst_ref=dst, send_sem=send, recv_sem=recv,
        device_id=where, device_id_type=MESH)


def pair_kernel(push, corr, flags, push_in, corr_in, flags_in, send, recv):
    tm, core = lax.axis_index("tm"), lax.axis_index("sens")
    other = (tm, 1 - core)
    barrier = pltpu.get_barrier_semaphore()
    pl.semaphore_signal(barrier, inc=1, device_id=other, device_id_type=MESH)
    pl.semaphore_wait(barrier, 1)
    half = push.shape[0] // 2
    theirs = pl.ds(pl.multiple_of((1 - core) * half, half), half)
    copies = [
        remote(corr, corr_in, send.at[0], recv.at[0], other),
        remote(push.at[theirs], push_in, send.at[1], recv.at[1], other),
        remote(flags, flags_in, send.at[2], recv.at[2], other),
    ]
    for copy in copies:
        copy.start()
    for copy in copies:
        copy.wait()


def maps_kernel(seg_len, push, push_in, corr, corr_in, flags, flags_in, trans,
                powers, ends, local, chunk, tree):
    core = lax.axis_index("sens")
    segs = ends.shape[0]
    width = trans.shape[0]
    blocks = corr.shape[0]
    levels = seg_len.bit_length() - 1

    together = 8

    def several(i, carry):
        ks = [i * together + j for j in range(together)]
        here = [pl.ds(pl.multiple_of(k * seg_len, seg_len), seg_len) for k in ks]
        qs, vs = [], []
        for k, at in zip(ks, here):
            row = core * segs + k
            q = trans[...].T
            for g in range(blocks):
                q = q - flags[row, g] * corr[g] - flags_in[row, g] * corr_in[g]
            mine = pl.ds(pl.multiple_of(row * seg_len, seg_len), seg_len)
            qs.append(q)
            vs.append(push[mine] + push_in[at])
        for s in range(levels):
            ts = [mm(jnp.concatenate([q, v], axis=0), q) for q, v in zip(qs, vs)]
            for k, q in zip(ks, qs):
                powers[s, k] = q
            vs = [v + shift_down(t[width:], 1 << s) for t, v in zip(ts, vs)]
            qs = [t[:width] for t in ts]
        for k, at, q, v in zip(ks, here, qs, vs):
            local[at] = v
            ends[k] = q
            tree[k, :width] = q
            tree[k, width:] = jnp.broadcast_to(v[seg_len - 1:], (8, width))
        return carry

    lax.fori_loop(0, segs // together, several, 0)
    span = 1
    while span < segs:
        for k in range(0, segs, 2 * span):
            tree[k] = compose(tree[k], tree[k + span])
        span *= 2
    chunk[...] = tree[0]


def compose(first, second):
    width = second.shape[1]
    t = mm(first, second[:width])
    return jnp.concatenate([t[:width], t[width:] + second[width:]], axis=0)


def follow(x, step):
    width = step.shape[1]
    return mv(x, step[:width]) + step[width:]


def carry_kernel(n, chunk, start, entry, pair, chip, group, arrived, leaving, send, recv):
    tm, core = lax.axis_index("tm"), lax.axis_index("sens")
    place, mine = lax.rem(tm, GROUP), lax.div(tm, GROUP)
    groups = n // GROUP
    other = (tm, 1 - core)
    base = tm - place
    peers = [(base + lax.rem(place + k, GROUP), core) for k in range(1, GROUP)]
    barrier = pltpu.get_barrier_semaphore()
    chain = [(lax.rem(tm + by, n), core) for by in (GROUP, n - GROUP)]
    for peer in [other] + peers + chain:
        pl.semaphore_signal(barrier, inc=1, device_id=peer, device_id_type=MESH)
    pl.semaphore_wait(barrier, GROUP + 2)

    swap = remote(chunk, pair, send.at[0], recv.at[0], other)
    swap.start()
    swap.wait()
    own, their = chunk[...], pair[...]
    first = jnp.where(core == 0, own, their)
    chip[...] = compose(first, jnp.where(core == 0, their, own))
    copies = []
    for k, peer in enumerate(peers):
        copy = remote(chip, group.at[k], send.at[1 + k], recv.at[1 + k], peer)
        copy.start()
        copies.append(copy)
    for copy in copies:
        copy.wait()
    held = [chip[...]] + [group[k] for k in range(GROUP - 1)]
    ordered = []
    for p in range(GROUP):
        value = held[0]
        for k in range(1, GROUP):
            value = jnp.where(lax.rem(place - k + GROUP, GROUP) == p, held[k], value)
        ordered.append(value)
    low, high = compose(ordered[0], ordered[1]), compose(ordered[2], ordered[3])
    whole = compose(low, high)
    hand = remote(leaving, arrived, send.at[GROUP], recv.at[GROUP], (tm + GROUP, core))

    @pl.when(mine == 0)
    def _():
        arrived[...] = start[...]

    @pl.when(mine > 0)
    def _():
        remote(leaving, arrived, send.at[GROUP], recv.at[GROUP], (tm - GROUP, core)).wait_recv()

    x = arrived[...]
    leaving[...] = follow(x, whole)

    @pl.when(mine < groups - 1)
    def _():
        hand.start()

    x = jnp.where(place >= 2, follow(x, low), x)
    before = jnp.where(place >= 2, ordered[2], ordered[0])
    x = jnp.where(lax.rem(place, 2) == 1, follow(x, before), x)
    entry[...] = jnp.where(core == 1, follow(x, first), x)

    @pl.when(mine < groups - 1)
    def _():
        hand.wait_send()


def filter_kernel(n, seg_len, entry, powers, ends, local, trans, smooth,
                  drive_scan, gains, shift, final, states, filtered):
    levels, segs = powers.shape[:2]
    width = trans.shape[0]
    rows = segs * seg_len

    x = entry[...]
    for k in range(segs):
        states[k] = x
        x = mv(x, ends[k]) + local[(k + 1) * seg_len - 1:(k + 1) * seg_len]

    together = 8

    def several(i, carry):
        ks = [i * together + j for j in range(together)]
        ws = [jnp.concatenate([states[k]] * (seg_len // 8), axis=0) for k in ks]
        ids = row_ids(ws[0].shape)
        for s in range(levels):
            ws = [jnp.where((ids // (1 << s)) % 2 == 1, mv(w, powers[s, k]), w)
                  for k, w in zip(ks, ws)]
        ws = [mv(w, powers[0, k]) for k, w in zip(ks, ws)]
        for k, w in zip(ks, ws):
            here = pl.ds(pl.multiple_of(k * seg_len, seg_len), seg_len)
            filtered[here] = local[here] + w
        return carry

    lax.fori_loop(0, segs // together, several, 0)
    f = filtered[...]
    ahead = mm_nt(f, trans[...])
    v = f - mm_nt(ahead, smooth[...])
    last = jnp.broadcast_to(ahead[rows - 1:], (8, width))
    final[...] = last
    p = smooth[...].T
    span, level = 1, 0
    while span < rows:
        gains[level] = p
        t = mm(jnp.concatenate([p, v], axis=0), p)
        v = v + shift_up(t[width:], span)
        p = t[:width]
        span, level = span * 2, level + 1
    gains[level] = p
    drive_scan[...] = v
    is_last = (lax.axis_index("tm") == n - 1) & (lax.axis_index("sens") == 1)
    s = jnp.broadcast_to(v[:1], (8, width))
    shift[...] = jnp.where(is_last, s + mm(last, p), s)


def smooth_kernel(n, drive_scan, gains, shift, final, out, entry, shifts, send, recv):
    tm, core = lax.axis_index("tm"), lax.axis_index("sens")
    chunks = 2 * n
    me = tm * 2 + core
    half, width = drive_scan.shape
    barrier = pltpu.get_barrier_semaphore()

    def place(k):
        c = lax.rem(me + k, chunks)
        return (lax.div(c, 2), lax.rem(c, 2))

    def greet(k, carry):
        pl.semaphore_signal(barrier, inc=1, device_id=place(k), device_id_type=MESH)
        return carry

    lax.fori_loop(1, chunks, greet, 0)
    pl.semaphore_wait(barrier, chunks - 1)

    def launch(k, carry):
        remote(shift, shifts.at[me], send.at[k], recv.at[me], place(k)).start()
        return carry

    lax.fori_loop(1, chunks, launch, 0)
    shifts[me] = shift[...]

    def land(k, carry):
        c = lax.rem(me + k, chunks)
        remote(shift, shifts.at[c], send.at[k], recv.at[c], place(k)).wait()
        return carry

    lax.fori_loop(1, chunks, land, 0)
    v = shifts[:, 0, :]
    levels = gains.shape[0] - 1
    p = gains[levels]
    span = 1
    while span < chunks:
        t = mm(jnp.concatenate([p, v], axis=0), p)
        v = v + shift_up(t[width:], span)
        p = t[:width]
        span *= 2
    x = jnp.sum(jnp.where(row_ids(v.shape) == me + 1, v, 0.0), axis=0, keepdims=True)
    x = jnp.where(me == chunks - 1, final[...], jnp.broadcast_to(x, (8, width)))
    after = jnp.where(row_ids(v.shape) == 2 * tm + 2, v, 0.0)
    entry[...] = jnp.broadcast_to(jnp.sum(after, axis=0, keepdims=True), (8, width))
    w = x
    ids = 7 - row_ids(w.shape)
    for s in range(3):
        w = jnp.where((ids // (1 << s)) % 2 == 1, mv(w, gains[s]), w)
    w = mv(w, gains[0])
    for s in range(3, levels):
        w = jnp.concatenate([mv(w, gains[s]), w], axis=0)
    mine = pl.ds(pl.multiple_of(core * half, half), half)
    out[mine] = drive_scan[...] + w
    swap = remote(out.at[mine], out.at[mine], send.at[0], recv.at[chunks], (tm, 1 - core))
    swap.start()
    swap.wait()


def stats_kernel(n, blocks, reducers, smoothed, entry, masked, flags, stats, smoothed_out):
    rows, width = smoothed.shape
    segs = flags.shape[0]
    seg_len = rows // segs
    sensors = masked.shape[1]
    tm, core = lax.axis_index("tm"), lax.axis_index("sens")
    x = smoothed[...]
    ids = row_ids((rows, width))
    weight = jnp.where((tm == n - 1) & (ids == rows - 1), 0.0, 1.0)
    prior = x * weight
    above = pltpu.roll(x, rows - 1, 0)
    above = jnp.where(ids == rows - 1, jnp.broadcast_to(entry[:1], (rows, width)), above)
    size = sensors // blocks
    cross = mm_tn(masked[...], x)
    smoothed_out[...] = x
    lag = jnp.concatenate([mm_tn(prior, x), mm_tn(above, prior)], axis=0)
    held = []
    for g in range(blocks):
        column = jnp.broadcast_to(flags[:, g:g + 1], (segs, width))
        step = jnp.broadcast_to(column[:, None, :], (segs, seg_len, width)).reshape(rows, width)
        held += [mm_tn(x * step, x), cross[g * size:(g + 1) * size]]
    sensor = jnp.concatenate(held, axis=0)
    lag_piece, piece = lag.shape[0] // reducers, sensor.shape[0] // reducers
    for r in range(reducers):
        at = r * (lag_piece + piece)
        stats[at:at + lag_piece] = lag[r * lag_piece:(r + 1) * lag_piece]
        stats[at + lag_piece:at + lag_piece + piece] = sensor[r * piece:(r + 1) * piece]


def sum_kernel(n, reducers, blocks, stats, lag, system, parts, total,
               send, recv, send2, recv2, send3, recv3):
    me, core = lax.axis_index("tm"), lax.axis_index("sens")
    step = n // reducers
    mine, reduces = me // step, me % step == 0
    lag_piece, piece = lag.shape[0] // reducers, system.shape[0] * blocks // reducers
    per_system = reducers // blocks
    groups = n // blocks
    both = lag_piece + piece
    barrier = pltpu.get_barrier_semaphore()

    def peer(k):
        return lax.rem(me + k, n)

    def greet(k, carry):
        pl.semaphore_signal(barrier, inc=1, device_id=(peer(k), core), device_id_type=MESH)
        return carry

    lax.fori_loop(1, n, greet, 0)
    pl.semaphore_wait(barrier, n - 1)

    def part_of(c):
        return stats.at[pl.ds(pl.multiple_of(c * both, both), both)]

    def give(k):
        c = lax.rem(mine + k, reducers)
        return remote(part_of(c), parts.at[me], send.at[k], recv.at[me], (c * step, core))

    def scatter(k, carry):
        give(k).start()
        return carry

    def sent(k, carry):
        give(k).wait_send()
        return carry

    def land(k, carry):
        c = peer(k)
        remote(part_of(0), parts.at[c], send.at[0], recv.at[c], (c, core)).wait_recv()
        return carry

    lax.fori_loop(1, reducers, scatter, 0)
    if step > 1:
        @pl.when(me % step != 0)
        def _():
            give(0).start()

    task, slot = mine // per_system, mine % per_system
    lag_at = pl.ds(pl.multiple_of(mine * lag_piece, lag_piece), lag_piece)
    system_at = pl.ds(pl.multiple_of(slot * piece, piece), piece)
    lag_part, system_part = total.at[pl.ds(0, lag_piece)], total.at[pl.ds(lag_piece, piece)]

    def tell(k):
        return remote(lag_part, lag.at[lag_at], send2.at[k], recv2.at[mine], (peer(k), core))

    def place(g):
        return lax.rem(me // blocks + g, groups) * blocks + task

    def hand(g):
        return remote(system_part, system.at[system_at], send3.at[g], recv3.at[slot], (place(g), core))

    @pl.when(reduces)
    def _():
        lax.fori_loop(1, n, land, 0)
        parts[me] = part_of(mine)[...]
        total[...] = jnp.sum(parts[...], axis=0)
        lag[lag_at] = total[:lag_piece]

        def spread(g, carry):
            @pl.when(place(g) != me)
            def _():
                hand(g).start()
            return carry

        lax.fori_loop(0, groups, spread, 0)

        @pl.when(me % blocks == task)
        def _():
            system[system_at] = total[lag_piece:]

        def announce(k, carry):
            tell(k).start()
            return carry

        lax.fori_loop(1, n, announce, 0)

    def take(j, carry):
        @pl.when((me % blocks * per_system + j) * step != me)
        def _():
            remote(system_part, system.at[pl.ds(pl.multiple_of(j * piece, piece), piece)],
                   send3.at[0], recv3.at[j], (peer(1), core)).wait_recv()
        return carry

    lax.fori_loop(0, per_system, take, 0)

    def hear(r, carry):
        @pl.when(r * step != me)
        def _():
            remote(lag_part, lag.at[pl.ds(pl.multiple_of(r * lag_piece, lag_piece), lag_piece)],
                   send2.at[0], recv2.at[r], (peer(1), core)).wait_recv()
        return carry

    lax.fori_loop(0, reducers, hear, 0)
    lax.fori_loop(1, reducers, sent, 0)
    if step > 1:
        @pl.when(me % step != 0)
        def _():
            give(0).wait_send()

    @pl.when(reduces)
    def _():
        def told(k, carry):
            tell(k).wait_send()
            return carry

        def handed(g, carry):
            @pl.when(place(g) != me)
            def _():
                hand(g).wait_send()
            return carry

        lax.fori_loop(1, n, told, 0)
        lax.fori_loop(0, groups, handed, 0)


def share_kernel(blocks, solved, new_sensing, send, recv):
    me, core = lax.axis_index("tm"), lax.axis_index("sens")
    size = solved.shape[0]
    task = lax.rem(me, blocks)
    base = me - task
    barrier = pltpu.get_barrier_semaphore()
    peers = [(base + lax.rem(task + k, blocks), core) for k in range(1, blocks)]
    for peer in peers:
        pl.semaphore_signal(barrier, inc=1, device_id=peer, device_id_type=MESH)
    pl.semaphore_wait(barrier, blocks - 1)

    def at(t):
        return pl.ds(pl.multiple_of(t * size, size), size)

    for k, peer in enumerate(peers):
        remote(solved, new_sensing.at[at(task)], send.at[k], recv.at[k], peer).start()
    new_sensing[at(task)] = solved[...]
    for k, peer in enumerate(peers):
        source = lax.rem(task - k - 1 + blocks, blocks)
        remote(solved, new_sensing.at[at(source)], send.at[k], recv.at[k], peer).wait()


def inverse_factor(a):
    count, size = a.shape[:2]
    shape = (count, size, 2 * size)
    wide = (count, 1, 2 * size)
    rows = lax.broadcasted_iota(jnp.int32, shape, 1)
    cols = lax.broadcasted_iota(jnp.int32, shape, 2)
    a = jnp.concatenate([a, jnp.where(rows + size == cols, 1.0, 0.0)[:, :, size:]], axis=2)
    scale = jnp.zeros(shape, F32)
    for k in range(0, size, TOGETHER):
        own = range(TOGETHER)
        pivot = [[jnp.broadcast_to(a[:, k + i:k + i + 1, k + j:k + j + 1], wide) if j >= i else None
                  for j in own] for i in own]
        r = [a[:, k + i:k + i + 1, :] for i in own]
        c = [jnp.broadcast_to(a[:, :, k + i:k + i + 1], shape) for i in own]
        for i in own:
            inv = 1.0 / pivot[i][i]
            scale = jnp.where(rows == k + i, inv, scale)
            for j in range(i + 1, TOGETHER):
                m = pivot[i][j] * inv
                for l in range(j, TOGETHER):
                    pivot[j][l] = pivot[j][l] - m * pivot[i][l]
                r[j] = r[j] - m * r[i]
                c[j] = c[j] - m * c[i]
            a = a - jnp.where(rows > k + i, c[i] * inv, 0.0) * r[i]
    return (a * jnp.sqrt(scale))[:, :, size:]


def solve_kernel(ridge, lag, system, new_transition, solved):
    width = lag.shape[1]
    size = solved.shape[0]
    eye = jnp.where(
        row_ids((width, width)) == lax.broadcasted_iota(jnp.int32, (width, width), 1), ridge, 0.0)
    left = system[width:].T
    left = jnp.concatenate([left] * (width // size), axis=1)
    rest = [jnp.concatenate([lag[:width] + eye, lag[width:].T], axis=1),
            jnp.concatenate([system[:width] + eye, left], axis=1)]
    both = range(2)
    steps = width // PIVOT
    inverses, panels = [], []
    for j in range(steps):
        lo, hi = j * PIVOT, (j + 1) * PIVOT
        inv = inverse_factor(jnp.stack([rest[s][:PIVOT, lo:hi] for s in both]))
        panel = [mm(inv[s], rest[s][:PIVOT]) for s in both]
        inverses.append(inv)
        panels.append(panel)
        if hi < width:
            rest = [rest[s][PIVOT:] - mm_tn(panel[s][:, :width], panel[s])[hi:] for s in both]
    x = [None, None]
    for j in reversed(range(steps)):
        hi = (j + 1) * PIVOT
        for s in both:
            rhs = panels[j][s][:, width:]
            if x[s] is not None:
                full = jnp.concatenate([jnp.zeros((hi, width), F32), x[s]], axis=0)
                rhs = rhs - mm(panels[j][s][:, :width], full)
            piece = mm_tn(inverses[j][s], rhs)
            x[s] = piece if x[s] is None else jnp.concatenate([piece, x[s]], axis=0)
    new_transition[...] = x[0].T
    solved[...] = x[1].T[:size]


def on_device(n, telemetry, present, transition, sensing, filter_gain, smooth_gain, initial_state):
    width = transition.shape[0]
    rows, sensors = telemetry.shape
    segs, blocks = present.shape
    seg_len = rows // segs
    half, half_segs = rows // 2, segs // 2
    dma = pltpu.SemaphoreType.DMA
    masked, push, corr, flags, transition, smooth_gain, start = vmem_call(
        push_kernel,
        (shaped(rows, sensors), shaped(rows, width), shaped(blocks, width, width),
         shaped(segs, 128), shaped(width, width), shaped(width, width), shaped(8, width)),
        in_specs=in_vmem(7),
    )(telemetry, present.T, transition, sensing, filter_gain, smooth_gain, initial_state[None])
    push_in, corr_in, flags_in = vmem_call(
        pair_kernel,
        (shaped(half, width), shaped(blocks, width, width), shaped(segs, 128)),
        [dma((3,)), dma((3,))],
        in_vmem(3), remote=1,
    )(push, corr, flags)
    levels = seg_len.bit_length() - 1
    scalars = pl.BlockSpec(memory_space=pltpu.SMEM)
    powers, ends, local, chunk = vmem_call(
        functools.partial(maps_kernel, seg_len),
        (shaped(levels, half_segs, width, width), shaped(half_segs, width, width),
         shaped(half, width), shaped(width + 8, width)),
        [VMEM((half_segs, width + 8, width), F32)],
        in_vmem(4) + [scalars, scalars] + in_vmem(1),
    )(push, push_in, corr, corr_in, flags, flags_in, transition)
    entry = vmem_call(
        functools.partial(carry_kernel, n),
        shaped(8, width),
        [VMEM((width + 8, width), F32), VMEM((width + 8, width), F32),
         VMEM((GROUP - 1, width + 8, width), F32), VMEM((8, width), F32), VMEM((8, width), F32),
         dma((GROUP + 1,)), dma((GROUP + 1,))],
        in_vmem(2), remote=2,
    )(chunk, start)
    back_levels = half.bit_length() - 1
    drive_scan, gains, shift, final = vmem_call(
        functools.partial(filter_kernel, n, seg_len),
        (shaped(half, width), shaped(back_levels + 1, width, width), shaped(8, width),
         shaped(8, width)),
        [VMEM((half_segs, 8, width), F32), VMEM((half, width), F32)],
        in_vmem(6),
    )(entry, powers, ends, local, transition, smooth_gain)
    smoothed, entry_back = vmem_call(
        functools.partial(smooth_kernel, n),
        (shaped(rows, width), shaped(8, width)),
        [VMEM((2 * n, 8, width), F32), dma((2 * n,)), dma((2 * n + 1,))],
        in_vmem(4), remote=3,
    )(drive_scan, gains, shift, final)
    size = sensors // blocks
    reducers = min(n, REDUCERS)
    high = 2 * width + blocks * (width + size)
    stats, smoothed = vmem_call(
        functools.partial(stats_kernel, n, blocks, reducers),
        (shaped(high, width), shaped(rows, width)),
        in_specs=in_vmem(4),
    )(smoothed, entry_back, masked, flags)
    lag, system = vmem_call(
        functools.partial(sum_kernel, n, reducers, blocks),
        (shaped(2 * width, width), shaped(width + size, width)),
        [VMEM((n, high // reducers, width), F32), VMEM((high // reducers, width), F32),
         dma((reducers,)), dma((n,)), dma((n,)), dma((reducers,)),
         dma((n // blocks,)), dma((reducers // blocks,))],
        in_vmem(1), remote=4,
    )(stats)
    new_transition, solved = vmem_call(
        functools.partial(solve_kernel, RIDGE * rows * n),
        (shaped(width, width), shaped(size, width)),
        in_specs=in_vmem(2),
    )(lag, system)
    new_sensing = vmem_call(
        functools.partial(share_kernel, blocks),
        shaped(sensors, width),
        [dma((blocks - 1,)), dma((blocks - 1,))],
        in_vmem(1), remote=5,
    )(solved)
    return (new_transition, new_sensing, smoothed)


def solution(mesh):
    placed = (P("tm", "sens"), P("tm", "sens"), P(), P("sens", None), P(None, "sens"), P(), P())
    return jax.shard_map(
        functools.partial(on_device, mesh.shape["tm"]),
        mesh=mesh,
        in_specs=placed,
        out_specs=(P(), P("sens", None), P("tm", None)),
        check_vma=False,
    )
```
